128 devices in a mesh: pts: 64 (over z, y, x), head: 2 (over core).
Axes of the slice: x: 4, y: 4, z: 4, core: 2. Of those that a mesh axis runs over, the one named last changes fastest.
Arguments:
- points: bfloat16 [64, 262144], P(None, 'pts'), may hold values from -64 to 64
- counts: int32 [64], P('pts'), may hold values from 1 to 4096, 196608 in all
- latents_init: bfloat16 [512, 768], P('head'), may hold values from -6 to 6
- enc_key_w: bfloat16 [64, 768], replicated, may hold values from -0.75 to 0.75
- enc_val_w: bfloat16 [64, 768], replicated, may hold values from -0.75 to 0.75
- lat_weights: bfloat16 [7, 768, 768], P(None, 'head'), may hold values from -0.21875 to 0.21875
- up_w: bfloat16 [768, 3072], P(None, 'head'), may hold values from -0.21875 to 0.21875
- down_w: bfloat16 [3072, 768], P('head'), may hold values from -0.109375 to 0.109375
- query_w: bfloat16 [64, 768], replicated, may hold values from -0.75 to 0.75
- class_w: bfloat16 [768, 16], replicated, may hold values from -0.21875 to 0.21875
Outputs:
- logits: float32 [16, 262144], P(None, ('pts', 'head'))
The draws below stay inside these ranges and needn't reach their ends.
Inputs may be any that keep to these rules, and one draw needn't show every extreme that they name: `counts`: every shard has at least one live point and one shard has exactly 4096.
All inputs are finite; a program needn't handle non-finite values.
Results may differ from the reference program's by a relative error of at most 0.025.
Values may be sent and summed in bfloat16 or wider, within the bound.
No kernel may reach another device: no remote copies, remote signals or barrier semaphores. Data moves between devices by JAX's collectives and lax.ppermute only.
A program may use at most 192 MiB of HBM per device.

```python
import math
import jax
import jax.numpy as jnp
import numpy as np
from jax import lax

C = 64
D = 768
HEADS = 12
L = 512
FF = 3072
CLASSES = 16
P_DEV = 4096
SHARDS = 64
NPTS = 262144
N_PTS = 64
N_HEAD = 2


def draw_points(key, part):
    key = jax.random.fold_in(key, 11)
    first = jax.random.fold_in(key, 0)
    values = jax.random.normal(first, (C, NPTS))
    return jnp.clip(values, -64.0, 64.0).astype(jnp.bfloat16)


def block_levels(rng, shape, cuts, smallest, largest):
    gain, own = 1.0, jax.random.fold_in(rng, 6)
    for dim, parts in cuts:
        steps = jnp.exp(jax.random.uniform(jax.random.fold_in(own, dim), (parts,), jnp.float32, smallest / len(cuts), largest / len(cuts)))
        gain = gain * jnp.repeat(steps, shape[dim] // parts).reshape([-1 if axis == dim else 1 for axis in range(len(shape))])
    return gain


def split_up(number_of, total, reach, slope):
    weights = [(1 << 20) // math.isqrt(rank ** slope) + 1 for rank in range(2, number_of + 1)]
    rest, holding = total - reach - (number_of - 1), [1] * (number_of - 1)
    while rest > 0:
        candidates = [i for i in range(number_of - 1) if holding[i] < reach]
        mass, remaining = sum([weights[i] for i in candidates]), rest
        for i in candidates:
            more = min(reach - holding[i], max(1, remaining * weights[i] // mass), rest)
            holding[i] = holding[i] + more
            rest = rest - more
    return np.array([reach] + holding)


def uneven(key, amount, total, bound, lean):
    if amount == 2:
        one = jax.random.randint(key, (), max(1, total - bound), min(bound, total - 1) + 1)
        return jnp.stack([one, total - one])
    tallies = jnp.asarray(split_up(amount, total, bound, lean), jnp.int32)
    twos = (amount - 1) // 2
    giver, sink = tallies[1:1 + 2 * twos:2], tallies[2:2 + 2 * twos:2]
    room = jnp.minimum(giver - 1, bound - sink)
    passed = jax.random.randint(jax.random.fold_in(key, 1), (twos,), 0, 1 << 20) % (room + 1)
    tallies = tallies.at[1:1 + 2 * twos:2].set(giver - passed).at[2:2 + 2 * twos:2].set(sink + passed)
    return tallies[jax.random.permutation(jax.random.fold_in(key, 2), amount)]


def centred(key, dims, spread, most, cuts=(), kind=jnp.bfloat16):
    array = spread * jax.random.normal(key, dims, jnp.float32)
    if cuts:
        array = array * block_levels(key, dims, cuts, -0.22, 0.18)
    return jnp.clip(array, -most, most).astype(kind)


def setup_inputs(seed: int = 0) -> dict:
    arg_keys = jax.random.split(jax.random.key(seed), 11)
    return {
        "points": draw_points(jax.random.fold_in(arg_keys[10], 71), 0),
        "counts": uneven(arg_keys[1], SHARDS, P_DEV * N_PTS * 3 // 4, P_DEV, 2).astype(jnp.int32),
        "latents_init": centred(arg_keys[2], (L, D), 1.0, 6.0, ((0, 2),)),
        "enc_key_w": centred(arg_keys[3], (C, D), C ** -0.5, 0.75),
        "enc_val_w": centred(arg_keys[4], (C, D), C ** -0.5, 0.75),
        "lat_weights": centred(arg_keys[5], (7, D, D), D ** -0.5, 0.21875, ((1, 2),)),
        "up_w": centred(arg_keys[6], (D, FF), D ** -0.5, 0.21875, ((1, 2),)),
        "down_w": centred(arg_keys[7], (FF, D), FF ** -0.5, 0.109375, ((0, 2),)),
        "query_w": centred(arg_keys[8], (C, D), C ** -0.5, 0.75),
        "class_w": centred(arg_keys[9], (D, CLASSES), D ** -0.5, 0.21875),
    }


def layer_norm(v):
    mean = lax.optimization_barrier(jnp.mean(v, axis=-1, keepdims=True))
    cent = v - mean
    var = lax.optimization_barrier(jnp.mean(cent * cent, axis=-1, keepdims=True))
    return cent * lax.rsqrt(var + 1e-05)

def reference(points, counts, latents_init, enc_key_w, enc_val_w, lat_weights, up_w, down_w, query_w, class_w):
    hsize = D // HEADS
    scale = hsize ** (-0.5)
    f32 = jnp.float32
    bf16 = jnp.bfloat16
    init32 = latents_init.astype(f32)
    equery = jnp.dot(layer_norm(init32).astype(bf16), lat_weights[0], preferred_element_type=f32).astype(bf16)
    equery = equery.astype(f32).reshape(L, HEADS, hsize)
    limits = jnp.repeat(counts, P_DEV)
    local = jnp.arange(NPTS, dtype=jnp.int32) % P_DEV
    valid = local < limits
    block = min(512, P_DEV)
    wkey = enc_key_w.astype(f32)
    wval = enc_val_w.astype(f32)

    def encode_step(carry, idx):
        top, total, accum = carry
        start = (idx * block).astype(jnp.int32)
        blk = lax.dynamic_slice_in_dim(points, start, block, 1).astype(f32)
        live = lax.dynamic_slice_in_dim(valid, start, block, 0)
        keys = jnp.einsum('cp,cd->pd', blk, wkey).astype(bf16).astype(f32).reshape(block, HEADS, hsize)
        vals = jnp.einsum('cp,cd->pd', blk, wval).astype(bf16).astype(f32).reshape(block, HEADS, hsize)
        scores = jnp.einsum('rhe,bhe->rhb', equery, keys) * scale
        scores = jnp.where(live[None, None, :], scores, -1e+30)
        newtop = jnp.maximum(top, lax.optimization_barrier(jnp.max(scores, axis=-1)))
        corr = jnp.exp(top - newtop)
        expo = jnp.exp(scores - newtop[..., None])
        total = total * corr + lax.optimization_barrier(jnp.sum(expo, axis=-1))
        weights = expo.astype(bf16).astype(f32)
        accum = accum * corr[..., None] + jnp.einsum('rhb,bhe->rhe', weights, vals)
        return ((newtop, total, accum), None)
    init_carry = (jnp.full((L, HEADS), -1e+30, f32), jnp.zeros((L, HEADS), f32), jnp.zeros((L, HEADS, hsize), f32))
    (top, total, accum), _ = lax.scan(encode_step, init_carry, jnp.arange(NPTS // block, dtype=jnp.int32))
    encoded = (init32 + (accum / total[..., None]).reshape(L, D)).astype(bf16)
    block_in = layer_norm(encoded.astype(f32)).astype(bf16)
    query = jnp.dot(block_in, lat_weights[1], preferred_element_type=f32).astype(bf16).astype(f32).reshape(L, HEADS, hsize)
    keyed = jnp.dot(block_in, lat_weights[2], preferred_element_type=f32).astype(bf16).astype(f32).reshape(L, HEADS, hsize)
    valued = jnp.dot(block_in, lat_weights[3], preferred_element_type=f32).astype(bf16).astype(f32).reshape(L, HEADS, hsize)
    scores = jnp.einsum('rhe,lhe->rhl', query, keyed) * scale
    scores = scores - lax.optimization_barrier(jnp.max(scores, axis=-1, keepdims=True))
    expo = jnp.exp(scores)
    weights = (expo / lax.optimization_barrier(jnp.sum(expo, axis=-1, keepdims=True))).astype(bf16).astype(f32)
    mixed = jnp.einsum('rhl,lhe->rhe', weights, valued).astype(bf16).reshape(L, D)
    latent2 = encoded.astype(f32) + jnp.dot(mixed, lat_weights[4], preferred_element_type=f32)
    mlp_in = layer_norm(latent2).astype(bf16)
    hidden = jax.nn.gelu(jnp.dot(mlp_in, up_w, preferred_element_type=f32)).astype(bf16)
    latents_out = (latent2 + jnp.dot(hidden, down_w, preferred_element_type=f32)).astype(bf16)
    dec_in = layer_norm(latents_out.astype(f32)).astype(bf16)
    dkeys = jnp.dot(dec_in, lat_weights[5], preferred_element_type=f32).astype(bf16).astype(f32).reshape(L, HEADS, hsize)
    dvals = jnp.dot(dec_in, lat_weights[6], preferred_element_type=f32).astype(bf16).astype(f32).reshape(L, HEADS, hsize)
    dblock = min(512, P_DEV // N_HEAD)
    wquery = query_w.astype(f32)
    wclass = class_w.astype(f32)

    def decode_block(idx):
        start = (idx * dblock).astype(jnp.int32)
        blk = lax.dynamic_slice_in_dim(points, start, dblock, 1).astype(f32)
        dq = jnp.einsum('cb,cd->bd', blk, wquery).astype(bf16).astype(f32).reshape(dblock, HEADS, hsize)
        sc = jnp.einsum('bhe,lhe->bhl', dq, dkeys) * scale
        sc = sc - lax.optimization_barrier(jnp.max(sc, axis=-1, keepdims=True))
        ex = jnp.exp(sc)
        wt = (ex / lax.optimization_barrier(jnp.sum(ex, axis=-1, keepdims=True))).astype(bf16).astype(f32)
        attended = jnp.einsum('bhl,lhe->bhe', wt, dvals).astype(bf16).astype(f32).reshape(dblock, D)
        return jnp.einsum('bd,dk->kb', attended, wclass)
    outs = lax.map(decode_block, jnp.arange(NPTS // dblock, dtype=jnp.int32))
    return jnp.transpose(outs, (1, 0, 2)).reshape(CLASSES, NPTS)
```

```python
import math

import jax
import jax.numpy as jnp
from jax import lax
from jax.experimental import pallas as pl
from jax.experimental.pallas import tpu as pltpu
from jax.sharding import PartitionSpec as P

HEADS = 12
HSIZE = 64
WIDTH = HEADS * HSIZE
PAIRS = HEADS // 2
OWNERS = 64
GROUPS = 32
LOG2_SCALE = HSIZE ** -0.5 * math.log2(math.e)
SAFE = 64.0
DEAD = -1e30

f32 = jnp.float32
bf16 = jnp.bfloat16
NT = (((1,), (1,)), ((), ()))
NN = (((1,), (0,)), ((), ()))


def dot(a, b, dims=NN):
    return lax.dot_general(a, b, dims, preferred_element_type=f32)


def norm(v):
    mean = jnp.mean(v, axis=-1, keepdims=True)
    cent = v - mean
    var = jnp.mean(cent * cent, axis=-1, keepdims=True)
    return cent * lax.rsqrt(var + 1e-05)


def split3(v):
    hi = v.astype(bf16).astype(f32)
    mid = (v - hi).astype(bf16).astype(f32)
    lo = (v - hi - mid).astype(bf16).astype(f32)
    return hi, mid, lo


def lanes(shape):
    return lax.broadcasted_iota(jnp.int32, shape, len(shape) - 1)


def block_diag(pair):
    lane = lanes(pair.shape)
    zero = jnp.zeros_like(pair)
    return jnp.concatenate([jnp.where(lane < 64, pair, zero), jnp.where(lane >= 64, pair, zero)], axis=0)


def vmem():
    return pl.BlockSpec(memory_space=pltpu.VMEM)


def smem():
    return pl.BlockSpec(memory_space=pltpu.SMEM)


def anywhere():
    return pl.BlockSpec(memory_space=pl.ANY)


def shape(dims, dtype=bf16):
    return jax.ShapeDtypeStruct(dims, dtype)


def params(mib):
    return pltpu.CompilerParams(vmem_limit_bytes=mib << 20)


def cost(flops, size, exps=0):
    return pl.CostEstimate(flops=flops, bytes_accessed=size, transcendentals=exps)


def prepare_kernel(count_ref, pts_any, lat_any, paug, pvt, normed, pn_ref, pts_ref, lat_ref, sem):
    slots = pts_ref.shape[1]
    count = count_ref[0]
    fetches = [pltpu.make_async_copy(pts_any, pts_ref, sem.at[0]), pltpu.make_async_copy(lat_any, lat_ref, sem.at[1])]
    for fetch in fetches:
        fetch.start()
    sub = lax.broadcasted_iota(jnp.int32, (64, slots), 0)
    col = lanes((64, slots))
    ext = jnp.where(sub < 3, 1.0, jnp.where((sub == 3) & (col >= count), DEAD, 0.0))
    paug[64:128, :] = ext.astype(bf16)
    fetches[0].wait()
    paug[0:64, :] = pts_ref[...]
    for i in range(slots // 128):
        blk = pts_ref[:, i * 128 : (i + 1) * 128].astype(f32)
        full = jnp.concatenate([blk, jnp.ones((64, 128), f32)], axis=0)
        pvt[i * 128 : (i + 1) * 128, :] = full.T.astype(bf16)
    fetches[1].wait()
    normed[...] = norm(lat_ref[...].astype(f32)).astype(bf16)
    pall = pts_ref[...].astype(f32)
    pn_ref[0] = jnp.max(jnp.sum(pall * pall, axis=0, keepdims=True))


def prepare(count, points, latents):
    slots = points.shape[1]
    return pl.pallas_call(
        prepare_kernel,
        out_shape=(shape((128, slots)), shape((slots, 128)), shape(latents.shape), shape((1,), f32)),
        in_specs=[smem(), anywhere(), anywhere()],
        out_specs=(vmem(), vmem(), vmem(), smem()),
        scratch_shapes=[
            pltpu.VMEM(points.shape, bf16),
            pltpu.VMEM(latents.shape, bf16),
            pltpu.SemaphoreType.DMA((2,)),
        ],
        compiler_params=params(16),
        cost_estimate=cost(0, 6 << 20),
        name="prepare",
    )(count, points, latents)


ROW_TILE = 384
PT_TILE = 512


def fold_kernel(pos_ref, pn_ref, normed, w_own, w_oth, key_any, paug, q_ref, qf, key_ref, sem):
    fetch = pltpu.make_async_copy(key_any, key_ref, sem)
    fetch.start()
    head = pos_ref[3]
    rows = OWNERS * 48
    slots = paug.shape[1]
    half = w_own.shape[0]
    lo, hi = normed[:, :half], normed[:, half:]
    first = head == 0
    equery = dot(jnp.where(first, lo, hi), w_own[...]) + dot(jnp.where(first, hi, lo), w_oth[...])
    equery = equery.astype(bf16)
    fetch.wait()
    lane8 = lanes((GROUPS, 8, 128))
    aug = jnp.where(lane8 == 67, 1.0, 0.0)
    for p in range(PAIRS):
        cols = slice(p * 128, (p + 1) * 128)
        x = dot(equery[:, cols], block_diag(key_ref[:, cols]), NT) * LOG2_SCALE
        x8 = x.reshape(GROUPS, 8, 128)
        y8 = pltpu.roll(x, 64, 1).reshape(GROUPS, 8, 128)
        s, q = p // 3, p % 3
        qf[:, s, 0, q] = jnp.where(lane8 < 64, x8, aug)
        qf[:, s, 1, q] = jnp.where(lane8 < 64, y8, aug)
    qall = qf[...].reshape(OWNERS, 48, 128)
    q_ref[...] = qall.astype(bf16)

    qsq = jnp.where(lanes(qall.shape) < 64, qall * qall, 0.0)
    qn = jnp.max(jnp.sum(qsq, axis=2, keepdims=True))

    @pl.when(qn * pn_ref[0] > SAFE * SAFE)
    def _():
        per = ROW_TILE // 48

        def tile(t, _):
            qt = q_ref[pl.ds(t * per, per)].reshape(ROW_TILE, 128)

            def chunk(j, top):
                start = pl.multiple_of(j * PT_TILE, PT_TILE)
                sc = dot(qt, paug[:, pl.ds(start, PT_TILE)])
                return jnp.maximum(top, jnp.max(sc, axis=1, keepdims=True))

            top = lax.fori_loop(0, slots // PT_TILE, chunk, jnp.full((ROW_TILE, 1), DEAD, f32))
            hi, mid, lo = split3(top)
            lane = lanes((ROW_TILE, 128))
            shift = jnp.where(lane == 64, hi, jnp.where(lane == 65, mid, lo))
            keep = (lane < 64) | (lane > 66)
            qt = jnp.where(keep, qt.astype(f32), -shift).astype(bf16)
            q_ref[pl.ds(t * per, per)] = qt.reshape(per, 48, 128)
            return 0

        lax.fori_loop(0, rows // ROW_TILE, tile, 0)


def fold(pos, pn, normed, w_own, w_oth, key_w, paug):
    return pl.pallas_call(
        fold_kernel,
        out_shape=shape((OWNERS, 48, 128)),
        in_specs=[smem(), smem(), vmem(), vmem(), vmem(), anywhere(), vmem()],
        out_specs=vmem(),
        scratch_shapes=[
            pltpu.VMEM((GROUPS, 2, 2, 3, 8, 128), f32),
            pltpu.VMEM(key_w.shape, bf16),
            pltpu.SemaphoreType.DMA,
        ],
        compiler_params=params(16),
        cost_estimate=cost(400 << 20, 4 << 20),
        name="fold",
    )(pos, pn, normed, w_own, w_oth, key_w, paug)


def encode_kernel(step, pos_ref, q_ref, paug, pvt, *rest):
    out_ref, acc = rest[-2:]
    slots = paug.shape[1]
    own = q_ref.shape[0] // 4
    per = ROW_TILE // 48
    quarter = lax.rem(pos_ref[0] + step, 4) * own

    def tile(t, _):
        qt = q_ref[pl.ds(quarter + t * per, per)].reshape(ROW_TILE, 128)
        total = jnp.zeros((ROW_TILE, 128), f32)
        for j in range(slots // PT_TILE):
            cols = slice(j * PT_TILE, (j + 1) * PT_TILE)
            ex = jnp.exp2(dot(qt, paug[:, cols])).astype(bf16)
            total = total + dot(ex, pvt[cols, :])
        acc[pl.ds(t * per, per)] = total.reshape(per, 2, 3, 8, 128)
        return 0

    lax.fori_loop(0, own // per, tile, 0)

    sums = acc[...]
    turned = pltpu.roll(sums[:, 1].reshape(own * 24, 128), 64, 1).reshape(own, 3, 8, 128)
    lane = lanes((own, 8, 128))
    parts = [jnp.where(lane < 64, sums[:, 0, q], turned[:, q]) for q in range(3)]
    extra = jnp.zeros((own, 8, 128), f32)
    for e in range(2):
        for q in range(3):
            extra = jnp.where(lane == 64 + 3 * e + q, sums[:, e, q], extra)
    out_ref[...] = jnp.concatenate(parts + [extra], axis=1).astype(bf16)

    shifts = -q_ref[pl.ds(quarter, own)].astype(f32)
    at = lanes(shifts.shape)
    shifted = jnp.max(jnp.where((at >= 64) & (at < 67), jnp.abs(shifts), 0.0)) > 0.0

    @pl.when(shifted)
    def _():
        tiles = shifts.reshape(own, 2, 3, 8, 128)
        more = extra
        for e in range(2):
            for q in range(3):
                for k in range(3):
                    one = tiles[:, e, q, :, 64 + k : 65 + k]
                    more = jnp.where(lane == 72 + 8 * k + 3 * e + q, one, more)
        out_ref[...] = jnp.concatenate(parts + [more], axis=1).astype(bf16)


def encode(step, pos, queries, paug, pvt, *after):
    own = OWNERS // 4
    return pl.pallas_call(
        lambda *refs: encode_kernel(step, *refs),
        out_shape=shape((own, 32, 128)),
        in_specs=[smem(), vmem(), vmem(), vmem()] + [anywhere()] * len(after),
        out_specs=vmem(),
        scratch_shapes=[pltpu.VMEM((own, 2, 3, 8, 128), f32)],
        compiler_params=params(16),
        cost_estimate=cost(768 * 4096 * 1024, 3 << 20, 768 * 4096),
        name="encode",
    )(pos, queries, paug, pvt, *after)


def merged(refs, both):
    xs = [r[...].astype(f32) for r in refs]
    both[...] = (xs[0] + xs[1]) + (xs[2] + xs[3])
    exts = [x[:, 24:32, :] for x in xs]
    lane = lanes(exts[0].shape)
    inside = (lane >= 72) & (lane < 96)
    flag = jnp.max(sum(jnp.where(inside, jnp.abs(e), 0.0) for e in exts))

    @pl.when(flag > 0.0)
    def _():
        shifts = [pltpu.roll(e, 128 - 8, 2) + pltpu.roll(e, 128 - 16, 2) + pltpu.roll(e, 128 - 24, 2) for e in exts]
        top = jnp.maximum(jnp.maximum(shifts[0], shifts[1]), jnp.maximum(shifts[2], shifts[3]))
        total = jnp.zeros(lane.shape, f32)
        parts = [jnp.zeros(lane.shape, f32) for _ in range(3)]
        here = (lane >= 64) & (lane < 70)
        for x, e, s in zip(xs, exts, shifts):
            wt = jnp.where(here, jnp.exp2(s - top), 0.0)
            total = total + e * wt
            for q in range(3):
                fac = jnp.where(lane < 64, wt[:, :, 64 + q : 65 + q], wt[:, :, 67 + q : 68 + q])
                parts[q] = parts[q] + x[:, q * 8 : (q + 1) * 8, :] * fac
        for k, part in enumerate(split3(jnp.where(here, top, 0.0))):
            total = total + pltpu.roll(part, 8 * (k + 1), 2)
        both[...] = jnp.concatenate(parts + [total], axis=1)


def spread_kernel(axis, pos_ref, x0, x1, x2, x3, o0, o1, o2, o3, both):
    merged((x0, x1, x2, x3), both)
    n = o0.shape[0]
    for k, out in enumerate((o0, o1, o2, o3)):
        out[...] = both[pl.ds(lax.rem(pos_ref[axis] + k, 4) * n, n)].astype(bf16)


def spread(axis, pos, xs):
    n = xs[0].shape[0]
    return pl.pallas_call(
        lambda *refs: spread_kernel(axis, *refs),
        out_shape=(shape((n // 4, 32, 128)),) * 4,
        in_specs=[smem()] + [vmem()] * 4,
        out_specs=(vmem(),) * 4,
        scratch_shapes=[pltpu.VMEM((n, 32, 128), f32)],
        compiler_params=params(16),
        cost_estimate=cost(0, n << 17),
        name="spread",
    )(pos, *xs)


def mean_kernel(x0, x1, x2, x3, out_ref, both):
    merged((x0, x1, x2, x3), both)
    low = lanes((8, 128)) < 64
    ext = both[0, 24:32, :]
    parts = []
    for q in range(3):
        tot = jnp.where(low, ext[:, 64 + q : 65 + q], ext[:, 67 + q : 68 + q])
        parts.append(both[0, q * 8 : (q + 1) * 8, :] / tot)
    out_ref[0] = jnp.concatenate(parts, axis=0).astype(bf16)


def mean_of(xs):
    return pl.pallas_call(
        mean_kernel,
        out_shape=shape((1, 24, 128)),
        in_specs=[vmem()] * 4,
        out_specs=vmem(),
        scratch_shapes=[pltpu.VMEM((1, 32, 128), f32)],
        compiler_params=params(16),
        cost_estimate=cost(0, 1 << 17),
        name="mean",
    )(*xs)


def join_kernel(*refs):
    out = refs[-1]
    n = refs[0].shape[0]
    for k in range(4):
        out[k * n : (k + 1) * n] = refs[k][...]


def join(xs):
    n = xs[0].shape[0]
    return pl.pallas_call(
        join_kernel,
        out_shape=shape((4 * n, 24, 128)),
        in_specs=[vmem()] * 4,
        out_specs=vmem(),
        compiler_params=params(8),
        cost_estimate=cost(0, n << 15),
        name="join",
    )(*xs)


def latent_kernel(
    pos_ref, g0, g1, g2, g3, h0, h1, h2, h3, i_own, i_oth, val_ref, query_ref, class_ref,
    wl_own, wl_oth, up_own, up_oth, down_own, down_oth,
    at_ref, b_ref,
    spot, enc, mix,
):
    x0, y0, z0, head = pos_ref[0], pos_ref[1], pos_ref[2], pos_ref[3]
    rows = i_own.shape[0]
    half = wl_own.shape[1]
    first = head == 0

    for k, (gs, init) in enumerate((((g0, g1, g2, g3), i_own), ((h0, h1, h2, h3), i_oth))):
        for kx, g in enumerate(gs):
            part = g[...].astype(f32)
            for ky in range(4):
                for kz in range(4):
                    at = lax.rem(x0 + kx, 4) * 16 + lax.rem(y0 + ky, 4) * 4 + lax.rem(z0 + kz, 4)
                    spot[at] = part[ky * 4 + kz].reshape(3, 8, 128)
        mean = spot[...].reshape(GROUPS, 2, 3, 8, 128)
        for p in range(PAIRS):
            cols = slice(p * 128, (p + 1) * 128)
            part = mean[:, p // 3, p % 3].reshape(rows, 128).astype(bf16)
            val = dot(part, block_diag(val_ref[:, cols]))
            enc[k * rows : (k + 1) * rows, cols] = (init[:, cols].astype(f32) + val).astype(bf16)
    block_in = norm(enc[...].astype(f32)).astype(bf16)

    def proj(x, i):
        lo, hi = x[:, :half], x[:, half:]
        return dot(jnp.where(first, lo, hi), wl_own[i]) + dot(jnp.where(first, hi, lo), wl_oth[i])

    keys = proj(block_in, 2).astype(bf16)
    vals = proj(block_in, 3).astype(bf16)
    query = proj(block_in[:rows], 1).astype(bf16)
    ones = jnp.ones((2 * rows, 128), bf16)
    low = lanes((rows, 128)) < 64
    zero = jnp.zeros((rows, 128), bf16)
    for p in range(PAIRS):
        cols = slice(p * 128, (p + 1) * 128)
        qp = query[:, cols]
        both = jnp.concatenate([jnp.where(low, qp, zero), jnp.where(low, zero, qp)], axis=0)
        sc = dot(both, keys[:, cols], NT) * LOG2_SCALE
        ex = jnp.exp2(sc - jnp.max(sc, axis=-1, keepdims=True)).astype(bf16)
        res = dot(ex, jnp.concatenate([vals[:, cols], ones], axis=1))
        res = res[:, :128] / res[:, 128:]
        mix[:, cols] = jnp.where(low, res[:rows], res[rows:]).astype(bf16)
    latent2 = enc[:rows].astype(f32) + proj(mix[...], 4)
    mlp_in = norm(latent2).astype(bf16)
    hidden = []
    for up in (up_own, up_oth):
        x = dot(mlp_in, up[...])
        hid = 0.5 * x * (1.0 + jnp.tanh(math.sqrt(2.0 / math.pi) * (x + 0.044715 * (x * x * x))))
        hidden.append(hid.astype(bf16))
    latents_out = (latent2 + dot(hidden[0], down_own[...]) + dot(hidden[1], down_oth[...])).astype(bf16)
    dec_in = norm(latents_out.astype(f32)).astype(bf16)
    dkeys = proj(dec_in, 5).astype(bf16)
    for p in range(PAIRS):
        cols = slice(p * 128, (p + 1) * 128)
        at_ref[cols, :] = (dot(block_diag(query_ref[:, cols]), dkeys[:, cols], NT) * LOG2_SCALE).astype(bf16)
    dvals = proj(dec_in, 6).astype(bf16)
    classes = class_ref[...]
    lane = lanes(classes.shape)
    none = jnp.zeros_like(classes)
    blocks = [jnp.where((lane >= 64 * h) & (lane < 64 * h + 64), classes, none) for h in range(16)]
    b_ref[...] = dot(dvals, jnp.concatenate(blocks, axis=0), NT).astype(bf16)


LATENT_MIB = 20


def latent_block(pos, gs, hs, i_own, i_oth, val_w, query_w, class_t, weights):
    rows = i_own.shape[0]
    return pl.pallas_call(
        latent_kernel,
        out_shape=(shape((WIDTH, rows)), shape((rows, 256))),
        in_specs=[smem()] + [vmem()] * 19,
        out_specs=(vmem(), vmem()),
        scratch_shapes=[
            pltpu.VMEM((OWNERS, 3, 8, 128), f32),
            pltpu.VMEM((2 * rows, WIDTH), bf16),
            pltpu.VMEM((rows, WIDTH), bf16),
        ],
        compiler_params=params(LATENT_MIB),
        cost_estimate=cost(6 << 30, 20 << 20, 3 << 20),
        name="latent_block",
    )(pos, *gs, *hs, i_own, i_oth, val_w, query_w, class_t, *weights)


DEC_TILE = 512


def decode_kernel(pos_ref, pn_ref, pvt, at_own, at_oth, b_own, b_oth, out_ref, pt, amat, bmat, sem):
    share = out_ref.shape[1]
    rows = b_own.shape[0]
    start = pl.multiple_of(pos_ref[3] * share, share)
    fetch = pltpu.make_async_copy(pvt.at[pl.ds(start, share)], pt, sem)
    fetch.start()
    sub = lax.broadcasted_iota(jnp.int32, (64, 2 * rows), 0)
    lane = lanes((rows, 128))
    worst = jnp.zeros((1, rows), f32)
    for h in range(HEADS):
        amat[h, 64:128, :] = jnp.where((sub >= 3 * h) & (sub < 3 * h + 3), 1.0, 0.0).astype(bf16)
        for k, (a, b) in enumerate(((at_own, b_own), (at_oth, b_oth))):
            part = a[h * 64 : (h + 1) * 64, :]
            amat[h, 0:64, k * rows : (k + 1) * rows] = part
            part = part.astype(f32)
            worst = jnp.maximum(worst, jnp.sum(part * part, axis=0, keepdims=True))
            g = h // 8
            own = (lane >= 16 * (h % 8)) & (lane < 16 * (h % 8) + 16)
            vals = b[:, g * 128 : (g + 1) * 128]
            bmat[h, k * rows : (k + 1) * rows, 0:128] = jnp.where(own, vals, jnp.zeros_like(vals))
            bmat[h, k * rows : (k + 1) * rows, 128:256] = jnp.ones((rows, 128), bf16)
    fetch.wait()
    lane = lanes((DEC_TILE, 128))
    for j in range(share // DEC_TILE):
        at = slice(j * DEC_TILE, (j + 1) * DEC_TILE)
        pt[at, :] = jnp.where(lane < 64, pt[at, :], jnp.zeros((DEC_TILE, 128), bf16))

    @pl.when(jnp.max(worst) * pn_ref[0] > SAFE * SAFE)
    def _():
        def block(j, _):
            at = pl.ds(pl.multiple_of(j * DEC_TILE, DEC_TILE), DEC_TILE)
            pts = pt[at, :]
            new = pts.astype(f32)
            for h in range(HEADS):
                top = jnp.max(dot(pts, amat[h]), axis=1, keepdims=True)
                for k, part in enumerate(split3(top)):
                    new = jnp.where(lane == 64 + 3 * h + k, -part, new)
            pt[at, :] = new.astype(bf16)
            return 0

        lax.fori_loop(0, share // DEC_TILE, block, 0)

    for j in range(share // DEC_TILE):
        at = slice(j * DEC_TILE, (j + 1) * DEC_TILE)

        def one_head(h, total):
            ex = jnp.exp2(dot(pt[at, :], amat[h])).astype(bf16)
            res = dot(ex, bmat[h])
            return total + res[:, :128] / res[:, 128:]

        total = lax.fori_loop(0, HEADS, one_head, jnp.zeros((DEC_TILE, 128), f32), unroll=4)
        for turn in (64, 32, 16):
            total = total + pltpu.roll(total, turn, 1)
        out_ref[:, at] = total.T[0:16, :]


def decode(pos, pn, pvt, at_own, at_oth, b_own, b_oth):
    rows = b_own.shape[0]
    share = pvt.shape[0] // 2
    return pl.pallas_call(
        decode_kernel,
        out_shape=shape((16, share), f32),
        in_specs=[smem(), smem(), anywhere()] + [vmem()] * 4,
        out_specs=vmem(),
        scratch_shapes=[
            pltpu.VMEM((share, 128), bf16),
            pltpu.VMEM((HEADS, 128, 2 * rows), bf16),
            pltpu.VMEM((HEADS, 2 * rows, 256), bf16),
            pltpu.SemaphoreType.DMA,
        ],
        compiler_params=params(32),
        cost_estimate=cost(3 << 32, 8 << 20, 12 << 20),
        name="decode",
    )(pos, pn, pvt, at_own, at_oth, b_own, b_oth)


STRIDE = (1, 4, 16)


def shifted_by(x, axis, k):
    st = STRIDE[axis]
    perm = []
    for i in range(OWNERS):
        c = i // st % 4
        perm.append((i, i + ((c + k) % 4 - c) * st))
    return lax.ppermute(x, "pts", perm)


def gathered(x, axis):
    return [x] + [shifted_by(x, axis, -k) for k in (1, 2, 3)]


def per_device(
    points, counts, latents_init, enc_key_w, enc_val_w, lat_weights, up_w, down_w, query_w, class_w
):
    swap = [(0, 1), (1, 0)]

    def other(x):
        return lax.ppermute(x, "head", swap)

    me = lax.axis_index("pts")
    pos = jnp.stack([me % 4, me // 4 % 4, me // 16, lax.axis_index("head")]).astype(jnp.int32)
    w0_own = lat_weights[0]
    w0_oth = other(w0_own)
    paug, pvt, normed, pn = prepare(counts, points, latents_init)
    (normed, w0_oth), late = lax.optimization_barrier(
        ((normed, w0_oth), (lat_weights, up_w, down_w, latents_init))
    )
    wl_oth, up_oth, down_oth, i_oth = [other(w) for w in late]
    queries = fold(pos, pn, normed, w0_own, w0_oth, enc_key_w, paug)

    part2 = encode(2, pos, queries, paug, pvt)
    got2 = shifted_by(part2, 0, 2)
    part1 = encode(1, pos, queries, paug, pvt, part2)
    got1 = shifted_by(part1, 0, 1)
    part3 = encode(3, pos, queries, paug, pvt, part1, got2, i_oth)
    got3 = shifted_by(part3, 0, 3)
    part0 = encode(0, pos, queries, paug, pvt, part3, got1, wl_oth)
    parts = spread(1, pos, [part0, got1, got2, got3])
    parts = spread(2, pos, [parts[0]] + [shifted_by(parts[k], 1, k) for k in (1, 2, 3)])
    mean = mean_of([parts[0]] + [shifted_by(parts[k], 2, k) for k in (1, 2, 3)])

    plane = join(gathered(join(gathered(mean, 2)), 1))
    gs = gathered(plane, 0)
    hs = [other(g) for g in gs]

    weights = (lat_weights, wl_oth, up_w, up_oth, down_w, down_oth)
    at_own, b_own = latent_block(
        pos, gs, hs, latents_init, i_oth, enc_val_w, query_w, class_w.T, weights
    )
    return decode(pos, pn, pvt, at_own, other(at_own), b_own, other(b_own))


def solution(mesh):
    placed = (
        P(None, "pts"),
        P("pts"),
        P("head", None),
        P(),
        P(),
        P(None, "head", None),
        P(None, "head"),
        P("head", None),
        P(),
        P(),
    )
    return jax.shard_map(
        per_device, mesh=mesh, in_specs=placed, out_specs=P(None, ("pts", "head")), check_vma=False
    )
```

```python
import math

import jax
import jax.numpy as jnp
from jax import lax
from jax.experimental import pallas as pl
from jax.experimental.pallas import tpu as pltpu
from jax.sharding import PartitionSpec as P

HEADS = 12
HSIZE = 64
WIDTH = HEADS * HSIZE
PAIRS = HEADS // 2
HALF = WIDTH // 2
KEY, VAL, QUERY, CLASS = 0, 64, 128, 192
OWNERS = 64
GROUPS = 32
LOG2_SCALE = HSIZE ** -0.5 * math.log2(math.e)
SAFE = 64.0
DEAD = -1e30

f32 = jnp.float32
bf16 = jnp.bfloat16
NT = (((1,), (1,)), ((), ()))
NN = (((1,), (0,)), ((), ()))


def dot(a, b, dims=NN):
    return lax.dot_general(a, b, dims, preferred_element_type=f32)


def norm(v):
    mean = jnp.mean(v, axis=-1, keepdims=True)
    cent = v - mean
    var = jnp.mean(cent * cent, axis=-1, keepdims=True)
    return cent * lax.rsqrt(var + 1e-05)


def split3(v):
    hi = v.astype(bf16).astype(f32)
    mid = (v - hi).astype(bf16).astype(f32)
    lo = (v - hi - mid).astype(bf16).astype(f32)
    return hi, mid, lo


def lanes(shape):
    return lax.broadcasted_iota(jnp.int32, shape, len(shape) - 1)


def block_diag(pair):
    lane = lanes(pair.shape)
    zero = jnp.zeros_like(pair)
    return jnp.concatenate([jnp.where(lane < 64, pair, zero), jnp.where(lane >= 64, pair, zero)], axis=0)


def vmem():
    return pl.BlockSpec(memory_space=pltpu.VMEM)


def smem():
    return pl.BlockSpec(memory_space=pltpu.SMEM)


def anywhere():
    return pl.BlockSpec(memory_space=pl.ANY)


def shape(dims, dtype=bf16):
    return jax.ShapeDtypeStruct(dims, dtype)


def params(mib=28):
    return pltpu.CompilerParams(vmem_limit_bytes=mib << 20)


def cost(flops, size, exps=0):
    return pl.CostEstimate(flops=flops, bytes_accessed=size, transcendentals=exps)


def prepare_kernel(count_ref, pts_ref, pack_ref, paug, pvt, normed, pn_ref):
    slots = pts_ref.shape[1]
    count = count_ref[0]
    sub = lax.broadcasted_iota(jnp.int32, (64, slots), 0)
    col = lanes((64, slots))
    ext = jnp.where(sub < 3, 1.0, jnp.where((sub == 3) & (col >= count), DEAD, 0.0))
    paug[0:64, :] = pts_ref[...]
    paug[64:128, :] = ext.astype(bf16)
    for i in range(slots // 128):
        blk = pts_ref[:, i * 128 : (i + 1) * 128].astype(f32)
        full = jnp.concatenate([blk, jnp.ones((64, 128), f32)], axis=0)
        pvt[i * 128 : (i + 1) * 128, :] = full.T.astype(bf16)
    normed[...] = norm(pack_ref[HALF:, :].astype(f32)).astype(bf16)
    pall = pts_ref[...].astype(f32)
    pn_ref[0] = jnp.max(jnp.sum(pall * pall, axis=0, keepdims=True))


def prepare(count, points, pack):
    slots = points.shape[1]
    return pl.pallas_call(
        prepare_kernel,
        out_shape=(shape((128, slots)), shape((slots, 128)), shape((pack.shape[0] - HALF, WIDTH)), shape((1,), f32)),
        in_specs=[smem(), vmem(), vmem()],
        out_specs=(vmem(), vmem(), vmem(), smem()),
        compiler_params=params(),
        cost_estimate=cost(0, 6 << 20),
        name="prepare",
    )(count, points, pack)


ROW_TILE = 512
PT_TILE = 512


def encode_kernel(pos_ref, pn_ref, normed, pack_own, pack_oth, small, paug, pvt, out_ref, qf, qaug, acc):
    rows = qaug.shape[0]
    slots = paug.shape[1]

    lo, hi = normed[:, :HALF], normed[:, HALF:]
    first = pos_ref[0] == 0
    equery = dot(jnp.where(first, lo, hi), pack_own[:HALF, :]) + dot(jnp.where(first, hi, lo), pack_oth[:HALF, :])
    equery = equery.astype(bf16)
    lane8 = lanes((GROUPS, 8, 128))
    aug = jnp.where(lane8 == 67, 1.0, 0.0)
    for p in range(PAIRS):
        cols = slice(p * 128, (p + 1) * 128)
        x = dot(equery[:, cols], block_diag(small[KEY : KEY + 64, cols]), NT) * LOG2_SCALE
        x8 = x.reshape(GROUPS, 8, 128)
        y8 = pltpu.roll(x, 64, 1).reshape(GROUPS, 8, 128)
        s, q = p // 3, p % 3
        qf[0, :, s, q] = jnp.where(lane8 < 64, x8, aug)
        qf[1, :, s, q] = jnp.where(lane8 < 64, y8, aug)
    qall = qf[...].reshape(rows, 128)
    qaug[...] = qall.astype(bf16)

    sub = lax.broadcasted_iota(jnp.int32, (128, 128), 0)
    sums = dot((qall * qall).astype(bf16), jnp.where(sub < 64, 1.0, 0.0).astype(bf16))
    shifted = jnp.max(sums) * pn_ref[0] > SAFE * SAFE

    @pl.when(shifted)
    def _():
        def tile(t, _):
            base = pl.multiple_of(t * ROW_TILE, ROW_TILE)
            qt = qaug[pl.ds(base, ROW_TILE), :]

            def chunk(j, top):
                start = pl.multiple_of(j * PT_TILE, PT_TILE)
                sc = dot(qt, paug[:, pl.ds(start, PT_TILE)])
                return jnp.maximum(top, jnp.max(sc, axis=1, keepdims=True))

            top = lax.fori_loop(0, slots // PT_TILE, chunk, jnp.full((ROW_TILE, 1), DEAD, f32))
            hi, mid, lo = split3(top)
            lane = lanes((ROW_TILE, 128))
            shift = jnp.where(lane == 64, hi, jnp.where(lane == 65, mid, lo))
            keep = (lane < 64) | (lane > 66)
            qaug[pl.ds(base, ROW_TILE), :] = jnp.where(keep, qt.astype(f32), -shift).astype(bf16)
            return 0

        lax.fori_loop(0, rows // ROW_TILE, tile, 0)

    def tile(t, _):
        base = pl.multiple_of(t * ROW_TILE, ROW_TILE)
        qt = qaug[pl.ds(base, ROW_TILE), :]
        total = jnp.zeros((ROW_TILE, 128), f32)
        chunks = [slice(j * PT_TILE, (j + 1) * PT_TILE) for j in range(slots // PT_TILE)]
        coming = dot(qt, paug[:, chunks[0]])
        for j, cols in enumerate(chunks):
            sc = coming
            if j + 1 < len(chunks):
                coming = dot(qt, paug[:, chunks[j + 1]])
            total = total + dot(jnp.exp2(sc).astype(bf16), pvt[cols, :])
        acc[pl.ds(base, ROW_TILE), :] = total
        return 0

    lax.fori_loop(0, rows // ROW_TILE, tile, 0)

    sums = acc[...].reshape(2, OWNERS, 3, 8, 128)
    turned = pltpu.roll(acc[rows // 2 :, :], 64, 1).reshape(OWNERS, 3, 8, 128)
    lane = lanes((OWNERS, 8, 128))
    parts = [jnp.where(lane < 64, sums[0, :, q], turned[:, q]) for q in range(3)]
    extra = jnp.zeros((OWNERS, 8, 128), f32)
    for e in range(2):
        for q in range(3):
            extra = jnp.where(lane == 64 + 3 * e + q, sums[e, :, q], extra)
    out_ref[...] = jnp.concatenate(parts + [extra], axis=1).astype(bf16)

    @pl.when(shifted)
    def _():
        shifts = -qaug[...].astype(f32).reshape(2, OWNERS, 3, 8, 128)
        more = extra
        for e in range(2):
            for q in range(3):
                for k in range(3):
                    one = shifts[e, :, q, :, 64 + k : 65 + k]
                    more = jnp.where(lane == 72 + 8 * k + 3 * e + q, one, more)
        out_ref[...] = jnp.concatenate(parts + [more], axis=1).astype(bf16)


def encode(pos, pn, normed, pack_own, pack_oth, small, paug, pvt):
    slots = paug.shape[1]
    rows = normed.shape[0] * HEADS
    return pl.pallas_call(
        encode_kernel,
        out_shape=shape((OWNERS, 32, 128)),
        in_specs=[smem(), smem()] + [vmem()] * 6,
        out_specs=vmem(),
        scratch_shapes=[
            pltpu.VMEM((2, GROUPS, 2, 3, 8, 128), f32),
            pltpu.VMEM((rows, 128), bf16),
            pltpu.VMEM((rows, 128), f32),
        ],
        compiler_params=params(),
        cost_estimate=cost(rows * slots * 1024, 6 << 20, rows * slots),
        name="encode",
    )(pos, pn, normed, pack_own, pack_oth, small, paug, pvt)


def merge_kernel(x_ref, out_ref, both):
    x = x_ref[...].astype(f32)
    ext = x[:, 24:32, :]
    lane = lanes(ext.shape)
    flag = jnp.max(jnp.where((lane >= 72) & (lane < 96), jnp.abs(ext), 0.0))
    both[...] = jnp.sum(x, axis=0)

    @pl.when(flag > 0.0)
    def _():
        shift = pltpu.roll(ext, 128 - 8, 2) + pltpu.roll(ext, 128 - 16, 2) + pltpu.roll(ext, 128 - 24, 2)
        wt = jnp.exp2(shift - jnp.max(shift, axis=0, keepdims=True))
        wt = jnp.where((lane >= 64) & (lane < 70), wt, 0.0)
        both[24:32, :] = jnp.sum(ext * wt, axis=0)
        for q in range(3):
            fac = jnp.where(lane < 64, wt[:, :, 64 + q : 65 + q], wt[:, :, 67 + q : 68 + q])
            both[q * 8 : (q + 1) * 8, :] = jnp.sum(x[:, q * 8 : (q + 1) * 8, :] * fac, axis=0)

    low = lanes((8, 128)) < 64
    parts = []
    for q in range(3):
        tot = jnp.where(low, both[24:32, 64 + q : 65 + q], both[24:32, 67 + q : 68 + q])
        parts.append(both[q * 8 : (q + 1) * 8, :] / tot)
    mean = jnp.concatenate(parts, axis=0).astype(bf16)
    for k in range(out_ref.shape[0]):
        out_ref[k] = mean


def merge(parts, copies):
    return pl.pallas_call(
        merge_kernel,
        out_shape=shape((copies, 24, 128)),
        in_specs=[vmem()],
        out_specs=vmem(),
        scratch_shapes=[pltpu.VMEM((32, 128), f32)],
        compiler_params=params(),
        cost_estimate=cost(0, 1 << 20),
        name="merge",
    )(parts)


def latent_kernel(
    pos_ref, g_own, g_oth, pack_own, pack_oth, small,
    wl_own, wl_oth, up_own, up_oth, down_own, down_oth,
    at_ref, b_ref,
    enc, mix,
):
    rows = mix.shape[0]
    head = pos_ref[0]
    first = head == 0
    for k, (g, pack) in enumerate(((g_own, pack_own), (g_oth, pack_oth))):
        mean = g[...].astype(f32).reshape(GROUPS, 2, 3, 8, 128)
        for p in range(PAIRS):
            cols = slice(p * 128, (p + 1) * 128)
            part = mean[:, p // 3, p % 3].reshape(rows, 128).astype(bf16)
            val = dot(part, block_diag(small[VAL : VAL + 64, cols]))
            enc[k * rows : (k + 1) * rows, cols] = (pack[HALF:, cols].astype(f32) + val).astype(bf16)
    block_in = norm(enc[...].astype(f32)).astype(bf16)

    def proj(x, i):
        lo, hi = x[:, :HALF], x[:, HALF:]
        return dot(jnp.where(first, lo, hi), wl_own[i]) + dot(jnp.where(first, hi, lo), wl_oth[i])

    keys = proj(block_in, 2).astype(bf16)
    vals = proj(block_in, 3).astype(bf16)
    query = proj(block_in[:rows], 1).astype(bf16)
    ones = jnp.ones((2 * rows, 128), bf16)
    low = lanes((rows, 128)) < 64
    zero = jnp.zeros((rows, 128), bf16)
    for p in range(PAIRS):
        cols = slice(p * 128, (p + 1) * 128)
        qp = query[:, cols]
        both = jnp.concatenate([jnp.where(low, qp, zero), jnp.where(low, zero, qp)], axis=0)
        sc = dot(both, keys[:, cols], NT) * LOG2_SCALE
        ex = jnp.exp2(sc - jnp.max(sc, axis=-1, keepdims=True)).astype(bf16)
        res = dot(ex, jnp.concatenate([vals[:, cols], ones], axis=1))
        res = res[:, :128] / res[:, 128:]
        mix[:, cols] = jnp.where(low, res[:rows], res[rows:]).astype(bf16)
    latent2 = enc[:rows].astype(f32) + proj(mix[...], 4)
    mlp_in = norm(latent2).astype(bf16)
    hidden = []
    for up in (up_own, up_oth):
        x = dot(mlp_in, up[...])
        hid = 0.5 * x * (1.0 + jnp.tanh(math.sqrt(2.0 / math.pi) * (x + 0.044715 * (x * x * x))))
        hidden.append(hid.astype(bf16))
    latents_out = (latent2 + dot(hidden[0], down_own[...]) + dot(hidden[1], down_oth[...])).astype(bf16)
    dec_in = norm(latents_out.astype(f32)).astype(bf16)
    dkeys = proj(dec_in, 5).astype(bf16)
    for p in range(PAIRS):
        cols = slice(p * 128, (p + 1) * 128)
        at_ref[cols, :] = (dot(block_diag(small[QUERY : QUERY + 64, cols]), dkeys[:, cols], NT) * LOG2_SCALE).astype(bf16)
    dvals = proj(dec_in, 6).astype(bf16)
    classes = small[CLASS : CLASS + 16, :]
    lane = lanes(classes.shape)
    none = jnp.zeros_like(classes)
    blocks = [jnp.where((lane >= 64 * h) & (lane < 64 * h + 64), classes, none) for h in range(16)]
    b_ref[...] = dot(dvals, jnp.concatenate(blocks, axis=0), NT).astype(bf16)


def latent_block(pos, g_own, g_oth, pack_own, pack_oth, small, weights):
    rows = pack_own.shape[0] - HALF
    return pl.pallas_call(
        latent_kernel,
        out_shape=(shape((WIDTH, rows)), shape((rows, 256))),
        in_specs=[smem()] + [vmem()] * 11,
        out_specs=(vmem(), vmem()),
        scratch_shapes=[
            pltpu.VMEM((2 * rows, WIDTH), bf16),
            pltpu.VMEM((rows, WIDTH), bf16),
        ],
        compiler_params=params(),
        cost_estimate=cost(6 << 30, 20 << 20, 3 << 20),
        name="latent_block",
    )(pos, g_own, g_oth, pack_own, pack_oth, small, *weights)


DEC_TILE = 512


def decode_kernel(pos_ref, pn_ref, pts_ref, at_own, at_oth, b_own, b_oth, out_ref, pt, amat, bmat):
    share = out_ref.shape[1]
    rows = b_own.shape[0]
    for i in range(share // 128):
        start = pl.multiple_of(pos_ref[0] * share + i * 128, 128)
        blk = pts_ref[:, pl.ds(start, 128)].astype(f32)
        full = jnp.concatenate([blk, jnp.zeros((64, 128), f32)], axis=0)
        pt[i * 128 : (i + 1) * 128, :] = full.T.astype(bf16)
    sub = lax.broadcasted_iota(jnp.int32, (64, 2 * rows), 0)
    lane = lanes((rows, 128))
    worst = jnp.zeros((1, rows), f32)
    for h in range(HEADS):
        amat[h, 64:128, :] = jnp.where((sub >= 3 * h) & (sub < 3 * h + 3), 1.0, 0.0).astype(bf16)
        for k, (a, b) in enumerate(((at_own, b_own), (at_oth, b_oth))):
            part = a[h * 64 : (h + 1) * 64, :]
            amat[h, 0:64, k * rows : (k + 1) * rows] = part
            part = part.astype(f32)
            worst = jnp.maximum(worst, jnp.sum(part * part, axis=0, keepdims=True))
            g = h // 8
            own = (lane >= 16 * (h % 8)) & (lane < 16 * (h % 8) + 16)
            vals = b[:, g * 128 : (g + 1) * 128]
            bmat[h, k * rows : (k + 1) * rows, 0:128] = jnp.where(own, vals, jnp.zeros_like(vals))
            bmat[h, k * rows : (k + 1) * rows, 128:256] = jnp.ones((rows, 128), bf16)
    lane = lanes((DEC_TILE, 128))

    @pl.when(jnp.max(worst) * pn_ref[0] > SAFE * SAFE)
    def _():
        def block(j, _):
            at = pl.ds(pl.multiple_of(j * DEC_TILE, DEC_TILE), DEC_TILE)
            pts = pt[at, :]
            new = pts.astype(f32)
            for h in range(HEADS):
                top = jnp.max(dot(pts, amat[h]), axis=1, keepdims=True)
                for k, part in enumerate(split3(top)):
                    new = jnp.where(lane == 64 + 3 * h + k, -part, new)
            pt[at, :] = new.astype(bf16)
            return 0

        lax.fori_loop(0, share // DEC_TILE, block, 0)

    def block(j, _):
        at = pl.ds(pl.multiple_of(j * DEC_TILE, DEC_TILE), DEC_TILE)
        pts = pt[at, :]
        total = jnp.zeros((DEC_TILE, 128), f32)
        coming = dot(pts, amat[0])
        for h in range(HEADS):
            sc = coming
            if h + 1 < HEADS:
                coming = dot(pts, amat[h + 1])
            res = dot(jnp.exp2(sc).astype(bf16), bmat[h])
            total = total + res[:, :128] / res[:, 128:]
        for turn in (64, 32, 16):
            total = total + pltpu.roll(total, turn, 1)
        out_ref[:, at] = total.T[0:16, :]
        return 0

    lax.fori_loop(0, share // DEC_TILE, block, 0)


def decode(pos, pn, points, at_own, at_oth, b_own, b_oth):
    rows = b_own.shape[0]
    share = points.shape[1] // 2
    return pl.pallas_call(
        decode_kernel,
        out_shape=shape((16, share), f32),
        in_specs=[smem(), smem()] + [vmem()] * 5,
        out_specs=vmem(),
        scratch_shapes=[
            pltpu.VMEM((share, 128), bf16),
            pltpu.VMEM((HEADS, 128, 2 * rows), bf16),
            pltpu.VMEM((HEADS, 2 * rows, 256), bf16),
        ],
        compiler_params=params(),
        cost_estimate=cost(3 << 32, 8 << 20, 12 << 20),
        name="decode",
    )(pos, pn, points, at_own, at_oth, b_own, b_oth)


def per_device(
    points, counts, latents_init, enc_key_w, enc_val_w, lat_weights, up_w, down_w, query_w, class_w
):
    swap = [(0, 1), (1, 0)]

    def other(x):
        return lax.ppermute(x, "head", swap)

    pos = lax.axis_index("head").astype(jnp.int32).reshape(1)
    pack_own = jnp.concatenate([lat_weights[0], latents_init], axis=0)
    pack_oth = other(pack_own)
    small = jnp.concatenate([enc_key_w, enc_val_w, query_w, class_w.T], axis=0)
    paug, pvt, normed, pn = prepare(counts, points, pack_own)
    (pn, pack_oth), late = lax.optimization_barrier(((pn, pack_oth), (lat_weights, up_w, down_w)))
    wl_oth, up_oth, down_oth = [other(w) for w in late]
    part = encode(pos, pn, normed, pack_own, pack_oth, small, paug, pvt)

    parts = lax.all_to_all(part, "pts", 0, 0)
    g_own = lax.all_to_all(merge(parts, OWNERS), "pts", 0, 0)
    g_oth = other(g_own)

    weights = (lat_weights, wl_oth, up_w, up_oth, down_w, down_oth)
    at_own, b_own = latent_block(pos, g_own, g_oth, pack_own, pack_oth, small, weights)
    return decode(pos, pn, points, at_own, other(at_own), b_own, other(b_own))


def solution(mesh):
    placed = (
        P(None, "pts"),
        P("pts"),
        P("head", None),
        P(),
        P(),
        P(None, "head", None),
        P(None, "head"),
        P("head", None),
        P(),
        P(),
    )
    return jax.shard_map(
        per_device, mesh=mesh, in_specs=placed, out_specs=P(None, ("pts", "head")), check_vma=False
    )
```

```python
import math

import jax
import jax.numpy as jnp
from jax import lax
from jax.experimental import pallas as pl
from jax.experimental.pallas import tpu as pltpu
from jax.sharding import PartitionSpec as P

HEADS = 12
HSIZE = 64
WIDTH = HEADS * HSIZE
PAIRS = HEADS // 2
HALF = WIDTH // 2
KEY, VAL, QUERY, CLASS = 0, 64, 128, 192
OWNERS = 64
GROUPS = 32
LOG2_SCALE = HSIZE ** -0.5 * math.log2(math.e)
SAFE = 64.0
DEAD = -1e30

f32 = jnp.float32
bf16 = jnp.bfloat16
NT = (((1,), (1,)), ((), ()))
NN = (((1,), (0,)), ((), ()))


def dot(a, b, dims=NN):
    return lax.dot_general(a, b, dims, preferred_element_type=f32)


def norm(v):
    mean = jnp.mean(v, axis=-1, keepdims=True)
    cent = v - mean
    var = jnp.mean(cent * cent, axis=-1, keepdims=True)
    return cent * lax.rsqrt(var + 1e-05)


def split3(v):
    hi = v.astype(bf16).astype(f32)
    mid = (v - hi).astype(bf16).astype(f32)
    lo = (v - hi - mid).astype(bf16).astype(f32)
    return hi, mid, lo


def lanes(shape):
    return lax.broadcasted_iota(jnp.int32, shape, len(shape) - 1)


def block_diag(pair):
    lane = lanes(pair.shape)
    zero = jnp.zeros_like(pair)
    return jnp.concatenate([jnp.where(lane < 64, pair, zero), jnp.where(lane >= 64, pair, zero)], axis=0)


def vmem():
    return pl.BlockSpec(memory_space=pltpu.VMEM)


def smem():
    return pl.BlockSpec(memory_space=pltpu.SMEM)


def anywhere():
    return pl.BlockSpec(memory_space=pl.ANY)


def shape(dims, dtype=bf16):
    return jax.ShapeDtypeStruct(dims, dtype)


def params(mib=28):
    return pltpu.CompilerParams(vmem_limit_bytes=mib << 20)


def cost(flops, size, exps=0):
    return pl.CostEstimate(flops=flops, bytes_accessed=size, transcendentals=exps)


def prepare_kernel(count_ref, pts_ref, pack_ref, before, paug, pvt, normed, pn_ref):
    slots = pts_ref.shape[1]
    count = count_ref[0]
    sub = lax.broadcasted_iota(jnp.int32, (64, slots), 0)
    col = lanes((64, slots))
    ext = jnp.where(sub < 3, 1.0, jnp.where((sub == 3) & (col >= count), DEAD, 0.0))
    paug[0:64, :] = pts_ref[...]
    paug[64:128, :] = ext.astype(bf16)
    for i in range(slots // 128):
        blk = pts_ref[:, i * 128 : (i + 1) * 128].astype(f32)
        full = jnp.concatenate([blk, jnp.ones((64, 128), f32)], axis=0)
        pvt[i * 128 : (i + 1) * 128, :] = full.T.astype(bf16)
    normed[...] = norm(pack_ref[HALF:, :].astype(f32)).astype(bf16)
    pall = pts_ref[...].astype(f32)
    pn_ref[0] = jnp.max(jnp.sum(pall * pall, axis=0, keepdims=True))


def prepare(count, points, pack, before):
    slots = points.shape[1]
    return pl.pallas_call(
        prepare_kernel,
        out_shape=(shape((128, slots)), shape((slots, 128)), shape((pack.shape[0] - HALF, WIDTH)), shape((1,), f32)),
        in_specs=[smem(), vmem(), vmem(), anywhere()],
        out_specs=(vmem(), vmem(), vmem(), smem()),
        compiler_params=params(),
        cost_estimate=cost(0, 6 << 20),
        name="prepare",
    )(count, points, pack, before)


ROW_TILE = 512
PT_TILE = 512


def encode_kernel(pos_ref, pn_ref, normed, pack_own, pack_oth, small, paug, pvt, out_ref, qf, qaug, acc):
    rows = qaug.shape[0]
    slots = paug.shape[1]

    lo, hi = normed[:, :HALF], normed[:, HALF:]
    first = pos_ref[0] == 0
    equery = dot(jnp.where(first, lo, hi), pack_own[:HALF, :]) + dot(jnp.where(first, hi, lo), pack_oth[:HALF, :])
    equery = equery.astype(bf16)
    lane8 = lanes((GROUPS, 8, 128))
    aug = jnp.where(lane8 == 67, 1.0, 0.0)
    for p in range(PAIRS):
        cols = slice(p * 128, (p + 1) * 128)
        x = dot(equery[:, cols], block_diag(small[KEY : KEY + 64, cols]), NT) * LOG2_SCALE
        x8 = x.reshape(GROUPS, 8, 128)
        y8 = pltpu.roll(x, 64, 1).reshape(GROUPS, 8, 128)
        s, q = p // 3, p % 3
        qf[0, :, s, q] = jnp.where(lane8 < 64, x8, aug)
        qf[1, :, s, q] = jnp.where(lane8 < 64, y8, aug)
    qall = qf[...].reshape(rows, 128)
    qaug[...] = qall.astype(bf16)

    sub = lax.broadcasted_iota(jnp.int32, (128, 128), 0)
    sums = dot((qall * qall).astype(bf16), jnp.where(sub < 64, 1.0, 0.0).astype(bf16))
    shifted = jnp.max(sums) * pn_ref[0] > SAFE * SAFE

    @pl.when(shifted)
    def _():
        def tile(t, _):
            base = pl.multiple_of(t * ROW_TILE, ROW_TILE)
            qt = qaug[pl.ds(base, ROW_TILE), :]

            def chunk(j, top):
                start = pl.multiple_of(j * PT_TILE, PT_TILE)
                sc = dot(qt, paug[:, pl.ds(start, PT_TILE)])
                return jnp.maximum(top, jnp.max(sc, axis=1, keepdims=True))

            top = lax.fori_loop(0, slots // PT_TILE, chunk, jnp.full((ROW_TILE, 1), DEAD, f32))
            hi, mid, lo = split3(top)
            lane = lanes((ROW_TILE, 128))
            shift = jnp.where(lane == 64, hi, jnp.where(lane == 65, mid, lo))
            keep = (lane < 64) | (lane > 66)
            qaug[pl.ds(base, ROW_TILE), :] = jnp.where(keep, qt.astype(f32), -shift).astype(bf16)
            return 0

        lax.fori_loop(0, rows // ROW_TILE, tile, 0)

    def tile(t, _):
        base = pl.multiple_of(t * ROW_TILE, ROW_TILE)
        qt = qaug[pl.ds(base, ROW_TILE), :]
        total = jnp.zeros((ROW_TILE, 128), f32)
        for j in range(slots // PT_TILE):
            cols = slice(j * PT_TILE, (j + 1) * PT_TILE)
            ex = jnp.exp2(dot(qt, paug[:, cols])).astype(bf16)
            total = total + dot(ex, pvt[cols, :])
        acc[pl.ds(base, ROW_TILE), :] = total
        return 0

    lax.fori_loop(0, rows // ROW_TILE, tile, 0)

    sums = acc[...].reshape(2, OWNERS, 3, 8, 128)
    turned = pltpu.roll(acc[rows // 2 :, :], 64, 1).reshape(OWNERS, 3, 8, 128)
    lane = lanes((OWNERS, 8, 128))
    parts = [jnp.where(lane < 64, sums[0, :, q], turned[:, q]) for q in range(3)]
    extra = jnp.zeros((OWNERS, 8, 128), f32)
    for e in range(2):
        for q in range(3):
            extra = jnp.where(lane == 64 + 3 * e + q, sums[e, :, q], extra)
    out_ref[...] = jnp.concatenate(parts + [extra], axis=1).astype(bf16)

    @pl.when(shifted)
    def _():
        shifts = -qaug[...].astype(f32).reshape(2, OWNERS, 3, 8, 128)
        more = extra
        for e in range(2):
            for q in range(3):
                for k in range(3):
                    one = shifts[e, :, q, :, 64 + k : 65 + k]
                    more = jnp.where(lane == 72 + 8 * k + 3 * e + q, one, more)
        out_ref[...] = jnp.concatenate(parts + [more], axis=1).astype(bf16)


def encode(pos, pn, normed, pack_own, pack_oth, small, paug, pvt):
    slots = paug.shape[1]
    rows = normed.shape[0] * HEADS
    return pl.pallas_call(
        encode_kernel,
        out_shape=shape((OWNERS, 32, 128)),
        in_specs=[smem(), smem()] + [vmem()] * 6,
        out_specs=vmem(),
        scratch_shapes=[
            pltpu.VMEM((2, GROUPS, 2, 3, 8, 128), f32),
            pltpu.VMEM((rows, 128), bf16),
            pltpu.VMEM((rows, 128), f32),
        ],
        compiler_params=params(),
        cost_estimate=cost(rows * slots * 1024, 6 << 20, rows * slots),
        name="encode",
    )(pos, pn, normed, pack_own, pack_oth, small, paug, pvt)


def merge_kernel(x_ref, out_ref, both):
    x = x_ref[...].astype(f32)
    ext = x[:, 24:32, :]
    lane = lanes(ext.shape)
    flag = jnp.max(jnp.where((lane >= 72) & (lane < 96), jnp.abs(ext), 0.0))
    both[...] = jnp.sum(x, axis=0)

    @pl.when(flag > 0.0)
    def _():
        shift = pltpu.roll(ext, 128 - 8, 2) + pltpu.roll(ext, 128 - 16, 2) + pltpu.roll(ext, 128 - 24, 2)
        wt = jnp.exp2(shift - jnp.max(shift, axis=0, keepdims=True))
        wt = jnp.where((lane >= 64) & (lane < 70), wt, 0.0)
        both[24:32, :] = jnp.sum(ext * wt, axis=0)
        for q in range(3):
            fac = jnp.where(lane < 64, wt[:, :, 64 + q : 65 + q], wt[:, :, 67 + q : 68 + q])
            both[q * 8 : (q + 1) * 8, :] = jnp.sum(x[:, q * 8 : (q + 1) * 8, :] * fac, axis=0)

    low = lanes((8, 128)) < 64
    parts = []
    for q in range(3):
        tot = jnp.where(low, both[24:32, 64 + q : 65 + q], both[24:32, 67 + q : 68 + q])
        parts.append(both[q * 8 : (q + 1) * 8, :] / tot)
    mean = jnp.concatenate(parts, axis=0).astype(bf16)
    for k in range(out_ref.shape[0]):
        out_ref[k] = mean


def merge(parts, copies):
    return pl.pallas_call(
        merge_kernel,
        out_shape=shape((copies, 24, 128)),
        in_specs=[vmem()],
        out_specs=vmem(),
        scratch_shapes=[pltpu.VMEM((32, 128), f32)],
        compiler_params=params(),
        cost_estimate=cost(0, 1 << 20),
        name="merge",
    )(parts)


def latent_kernel(
    pos_ref, g_own, g_oth, pack_own, pack_oth, small,
    wl_own, wl_oth, up_own, up_oth, down_own, down_oth,
    at_ref, b_ref,
    enc, mix, wbuf, sem,
):
    rows = mix.shape[0]
    head = pos_ref[0]
    copies = {}
    for i in (2, 3, 1, 4, 5, 6):
        for k, (src, at) in enumerate(((wl_own, head), (wl_oth, 1 - head))):
            dst = wbuf.at[i - 1, pl.ds(pl.multiple_of(at * HALF, HALF), HALF)]
            copies[i, k] = pltpu.make_async_copy(src.at[i], dst, sem.at[i - 1, k])
            copies[i, k].start()
    for k, (g, pack) in enumerate(((g_own, pack_own), (g_oth, pack_oth))):
        mean = g[...].astype(f32).reshape(GROUPS, 2, 3, 8, 128)
        for p in range(PAIRS):
            cols = slice(p * 128, (p + 1) * 128)
            part = mean[:, p // 3, p % 3].reshape(rows, 128).astype(bf16)
            val = dot(part, block_diag(small[VAL : VAL + 64, cols]))
            enc[k * rows : (k + 1) * rows, cols] = (pack[HALF:, cols].astype(f32) + val).astype(bf16)
    block_in = norm(enc[...].astype(f32)).astype(bf16)

    def proj(x, i):
        for k in range(2):
            copies[i, k].wait()
        return dot(x, wbuf[i - 1])

    keys = proj(block_in, 2).astype(bf16)
    vals = proj(block_in, 3).astype(bf16)
    query = proj(block_in[:rows], 1).astype(bf16)
    ones = jnp.ones((2 * rows, 128), bf16)
    low = lanes((rows, 128)) < 64
    zero = jnp.zeros((rows, 128), bf16)
    for p in range(PAIRS):
        cols = slice(p * 128, (p + 1) * 128)
        qp = query[:, cols]
        both = jnp.concatenate([jnp.where(low, qp, zero), jnp.where(low, zero, qp)], axis=0)
        sc = dot(both, keys[:, cols], NT) * LOG2_SCALE
        ex = jnp.exp2(sc - jnp.max(sc, axis=-1, keepdims=True)).astype(bf16)
        res = dot(ex, jnp.concatenate([vals[:, cols], ones], axis=1))
        res = res[:, :128] / res[:, 128:]
        mix[:, cols] = jnp.where(low, res[:rows], res[rows:]).astype(bf16)
    latent2 = enc[:rows].astype(f32) + proj(mix[...], 4)
    mlp_in = norm(latent2).astype(bf16)
    hidden = []
    for up in (up_own, up_oth):
        x = dot(mlp_in, up[...])
        hid = 0.5 * x * (1.0 + jnp.tanh(math.sqrt(2.0 / math.pi) * (x + 0.044715 * (x * x * x))))
        hidden.append(hid.astype(bf16))
    latents_out = (latent2 + dot(hidden[0], down_own[...]) + dot(hidden[1], down_oth[...])).astype(bf16)
    dec_in = norm(latents_out.astype(f32)).astype(bf16)
    dkeys = proj(dec_in, 5).astype(bf16)
    for p in range(PAIRS):
        cols = slice(p * 128, (p + 1) * 128)
        at_ref[cols, :] = (dot(block_diag(small[QUERY : QUERY + 64, cols]), dkeys[:, cols], NT) * LOG2_SCALE).astype(bf16)
    dvals = proj(dec_in, 6).astype(bf16)
    classes = small[CLASS : CLASS + 16, :]
    lane = lanes(classes.shape)
    none = jnp.zeros_like(classes)
    blocks = [jnp.where((lane >= 64 * h) & (lane < 64 * h + 64), classes, none) for h in range(16)]
    b_ref[...] = dot(dvals, jnp.concatenate(blocks, axis=0), NT).astype(bf16)


def latent_block(pos, g_own, g_oth, pack_own, pack_oth, small, weights):
    rows = pack_own.shape[0] - HALF
    return pl.pallas_call(
        latent_kernel,
        out_shape=(shape((WIDTH, rows)), shape((rows, 256))),
        in_specs=[smem()] + [vmem()] * 5 + [anywhere()] * 2 + [vmem()] * 4,
        out_specs=(vmem(), vmem()),
        scratch_shapes=[
            pltpu.VMEM((2 * rows, WIDTH), bf16),
            pltpu.VMEM((rows, WIDTH), bf16),
            pltpu.VMEM((6, WIDTH, WIDTH), bf16),
            pltpu.SemaphoreType.DMA((6, 2)),
        ],
        compiler_params=params(),
        cost_estimate=cost(6 << 30, 20 << 20, 3 << 20),
        name="latent_block",
    )(pos, g_own, g_oth, pack_own, pack_oth, small, *weights)


DEC_TILE = 512


def decode_kernel(pos_ref, pn_ref, pts_ref, at_own, at_oth, b_own, b_oth, out_ref, pt, amat, bmat):
    share = out_ref.shape[1]
    rows = b_own.shape[0]
    for i in range(share // 128):
        start = pl.multiple_of(pos_ref[0] * share + i * 128, 128)
        blk = pts_ref[:, pl.ds(start, 128)].astype(f32)
        full = jnp.concatenate([blk, jnp.zeros((64, 128), f32)], axis=0)
        pt[i * 128 : (i + 1) * 128, :] = full.T.astype(bf16)
    sub = lax.broadcasted_iota(jnp.int32, (64, 2 * rows), 0)
    lane = lanes((rows, 128))
    worst = jnp.zeros((1, rows), f32)
    for h in range(HEADS):
        amat[h, 64:128, :] = jnp.where((sub >= 3 * h) & (sub < 3 * h + 3), 1.0, 0.0).astype(bf16)
        for k, (a, b) in enumerate(((at_own, b_own), (at_oth, b_oth))):
            part = a[h * 64 : (h + 1) * 64, :]
            amat[h, 0:64, k * rows : (k + 1) * rows] = part
            part = part.astype(f32)
            worst = jnp.maximum(worst, jnp.sum(part * part, axis=0, keepdims=True))
            g = h // 8
            own = (lane >= 16 * (h % 8)) & (lane < 16 * (h % 8) + 16)
            vals = b[:, g * 128 : (g + 1) * 128]
            bmat[h, k * rows : (k + 1) * rows, 0:128] = jnp.where(own, vals, jnp.zeros_like(vals))
            bmat[h, k * rows : (k + 1) * rows, 128:256] = jnp.ones((rows, 128), bf16)
    lane = lanes((DEC_TILE, 128))

    @pl.when(jnp.max(worst) * pn_ref[0] > SAFE * SAFE)
    def _():
        def block(j, _):
            at = pl.ds(pl.multiple_of(j * DEC_TILE, DEC_TILE), DEC_TILE)
            pts = pt[at, :]
            new = pts.astype(f32)
            for h in range(HEADS):
                top = jnp.max(dot(pts, amat[h]), axis=1, keepdims=True)
                for k, part in enumerate(split3(top)):
                    new = jnp.where(lane == 64 + 3 * h + k, -part, new)
            pt[at, :] = new.astype(bf16)
            return 0

        lax.fori_loop(0, share // DEC_TILE, block, 0)

    def block(j, _):
        at = pl.ds(pl.multiple_of(j * DEC_TILE, DEC_TILE), DEC_TILE)
        pts = pt[at, :]
        total = jnp.zeros((DEC_TILE, 128), f32)
        coming = dot(pts, amat[0])
        for h in range(HEADS):
            sc = coming
            if h + 1 < HEADS:
                coming = dot(pts, amat[h + 1])
            res = dot(jnp.exp2(sc).astype(bf16), bmat[h])
            total = total + res[:, :128] / res[:, 128:]
        for turn in (64, 32, 16):
            total = total + pltpu.roll(total, turn, 1)
        out_ref[:, at] = total.T[0:16, :]
        return 0

    lax.fori_loop(0, share // DEC_TILE, block, 0)


def decode(pos, pn, points, at_own, at_oth, b_own, b_oth):
    rows = b_own.shape[0]
    share = points.shape[1] // 2
    return pl.pallas_call(
        decode_kernel,
        out_shape=shape((16, share), f32),
        in_specs=[smem(), smem()] + [vmem()] * 5,
        out_specs=vmem(),
        scratch_shapes=[
            pltpu.VMEM((share, 128), bf16),
            pltpu.VMEM((HEADS, 128, 2 * rows), bf16),
            pltpu.VMEM((HEADS, 2 * rows, 256), bf16),
        ],
        compiler_params=params(),
        cost_estimate=cost(3 << 32, 8 << 20, 12 << 20),
        name="decode",
    )(pos, pn, points, at_own, at_oth, b_own, b_oth)


def per_device(
    points, counts, latents_init, enc_key_w, enc_val_w, lat_weights, up_w, down_w, query_w, class_w
):
    swap = [(0, 1), (1, 0)]

    def other(x):
        return lax.ppermute(x, "head", swap)

    pos = lax.axis_index("head").astype(jnp.int32).reshape(1)
    pack_own = jnp.concatenate([lat_weights[0], latents_init], axis=0)
    pack_oth = other(pack_own)
    small = jnp.concatenate([enc_key_w, enc_val_w, query_w, class_w.T], axis=0)
    paug, pvt, normed, pn = prepare(counts, points, pack_own, small)
    (pn, pack_oth), late = lax.optimization_barrier(((pn, pack_oth), (lat_weights, up_w, down_w)))
    wl_oth, up_oth, down_oth = [other(w) for w in late]
    part = encode(pos, pn, normed, pack_own, pack_oth, small, paug, pvt)

    parts = lax.all_to_all(part, "pts", 0, 0)
    g_own = lax.all_to_all(merge(parts, OWNERS), "pts", 0, 0)
    g_oth = other(g_own)

    weights = (lat_weights, wl_oth, up_w, up_oth, down_w, down_oth)
    at_own, b_own = latent_block(pos, g_own, g_oth, pack_own, pack_oth, small, weights)
    return decode(pos, pn, points, at_own, other(at_own), b_own, other(b_own))


def solution(mesh):
    placed = (
        P(None, "pts"),
        P("pts"),
        P("head", None),
        P(),
        P(),
        P(None, "head", None),
        P(None, "head"),
        P("head", None),
        P(),
        P(),
    )
    return jax.shard_map(
        per_device, mesh=mesh, in_specs=placed, out_specs=P(None, ("pts", "head")), check_vma=False
    )
```

```python
import math

import jax
import jax.numpy as jnp
from jax import lax
from jax.experimental import pallas as pl
from jax.experimental.pallas import tpu as pltpu
from jax.sharding import PartitionSpec as P

HEADS = 12
HSIZE = 64
WIDTH = HEADS * HSIZE
PAIRS = HEADS // 2
HALF = WIDTH // 2
KEY, VAL, QUERY, CLASS = 0, 64, 128, 192
OWNERS = 64
GROUPS = 32
LOG2_SCALE = HSIZE ** -0.5 * math.log2(math.e)
SAFE = 64.0
DEAD = -1e30

f32 = jnp.float32
bf16 = jnp.bfloat16
NT = (((1,), (1,)), ((), ()))
NN = (((1,), (0,)), ((), ()))


def dot(a, b, dims=NN):
    return lax.dot_general(a, b, dims, preferred_element_type=f32)


def norm(v):
    mean = jnp.mean(v, axis=-1, keepdims=True)
    cent = v - mean
    var = jnp.mean(cent * cent, axis=-1, keepdims=True)
    return cent * lax.rsqrt(var + 1e-05)


def split3(v):
    hi = v.astype(bf16).astype(f32)
    mid = (v - hi).astype(bf16).astype(f32)
    lo = (v - hi - mid).astype(bf16).astype(f32)
    return hi, mid, lo


def lanes(shape):
    return lax.broadcasted_iota(jnp.int32, shape, len(shape) - 1)


def block_diag(pair):
    lane = lanes(pair.shape)
    zero = jnp.zeros_like(pair)
    return jnp.concatenate([jnp.where(lane < 64, pair, zero), jnp.where(lane >= 64, pair, zero)], axis=0)


def vmem():
    return pl.BlockSpec(memory_space=pltpu.VMEM)


def smem():
    return pl.BlockSpec(memory_space=pltpu.SMEM)


def anywhere():
    return pl.BlockSpec(memory_space=pl.ANY)


def shape(dims, dtype=bf16):
    return jax.ShapeDtypeStruct(dims, dtype)


def params(mib=28):
    return pltpu.CompilerParams(vmem_limit_bytes=mib << 20)


def cost(flops, size, exps=0):
    return pl.CostEstimate(flops=flops, bytes_accessed=size, transcendentals=exps)


def prepare_kernel(count_ref, pts_ref, pack_ref, before, paug, pvt, normed, pn_ref):
    slots = pts_ref.shape[1]
    count = count_ref[0]
    sub = lax.broadcasted_iota(jnp.int32, (64, slots), 0)
    col = lanes((64, slots))
    ext = jnp.where(sub < 3, 1.0, jnp.where((sub == 3) & (col >= count), DEAD, 0.0))
    paug[0:64, :] = pts_ref[...]
    paug[64:128, :] = ext.astype(bf16)
    for i in range(slots // 128):
        blk = pts_ref[:, i * 128 : (i + 1) * 128].astype(f32)
        full = jnp.concatenate([blk, jnp.ones((64, 128), f32)], axis=0)
        pvt[i * 128 : (i + 1) * 128, :] = full.T.astype(bf16)
    normed[...] = norm(pack_ref[HALF:, :].astype(f32)).astype(bf16)
    pall = pts_ref[...].astype(f32)
    pn_ref[0] = jnp.max(jnp.sum(pall * pall, axis=0, keepdims=True))


def prepare(count, points, pack, before):
    slots = points.shape[1]
    return pl.pallas_call(
        prepare_kernel,
        out_shape=(shape((128, slots)), shape((slots, 128)), shape((pack.shape[0] - HALF, WIDTH)), shape((1,), f32)),
        in_specs=[smem(), vmem(), vmem(), anywhere()],
        out_specs=(vmem(), vmem(), vmem(), smem()),
        compiler_params=params(),
        cost_estimate=cost(0, 6 << 20),
        name="prepare",
    )(count, points, pack, before)


ROW_TILE = 1536
PT_TILE = 512


def encode_kernel(pos_ref, par_ref, pn_ref, normed, pack_own, pack_oth, small, paug, pvt, out_ref, q_ref, qf, qaug, acc):
    rows = qaug.shape[1]
    slots = paug.shape[1]
    keep = par_ref[0]

    lo, hi = normed[:, :HALF], normed[:, HALF:]
    first = pos_ref[0] == 0
    equery = dot(jnp.where(first, lo, hi), pack_own[:HALF, :]) + dot(jnp.where(first, hi, lo), pack_oth[:HALF, :])
    equery = equery.astype(bf16)
    lane8 = lanes((GROUPS, 8, 128))
    aug = jnp.where(lane8 == 67, 1.0, 0.0)
    for p in range(PAIRS):
        cols = slice(p * 128, (p + 1) * 128)
        x = dot(equery[:, cols], block_diag(small[KEY : KEY + 64, cols]), NT) * LOG2_SCALE
        x8 = x.reshape(GROUPS, 8, 128)
        y8 = pltpu.roll(x, 64, 1).reshape(GROUPS, 8, 128)
        s, q = p // 3, p % 3
        qf[s, 0, :, q] = jnp.where(lane8 < 64, x8, aug)
        qf[s, 1, :, q] = jnp.where(lane8 < 64, y8, aug)
    qall = qf[...].reshape(2 * rows, 128)
    qaug[...] = qall.astype(bf16).reshape(2, rows, 128)

    sub = lax.broadcasted_iota(jnp.int32, (128, 128), 0)
    sums = dot((qall * qall).astype(bf16), jnp.where(sub < 64, 1.0, 0.0).astype(bf16))
    shifted = jnp.max(sums) * pn_ref[0] > SAFE * SAFE

    @pl.when(shifted)
    def _():
        def half(t, _):
            qt = qaug[t]

            def chunk(j, top):
                start = pl.multiple_of(j * PT_TILE, PT_TILE)
                sc = dot(qt, paug[:, pl.ds(start, PT_TILE)])
                return jnp.maximum(top, jnp.max(sc, axis=1, keepdims=True))

            top = lax.fori_loop(0, slots // PT_TILE, chunk, jnp.full((rows, 1), DEAD, f32))
            hi, mid, lo = split3(top)
            lane = lanes((rows, 128))
            shift = jnp.where(lane == 64, hi, jnp.where(lane == 65, mid, lo))
            same = (lane < 64) | (lane > 66)
            qaug[t] = jnp.where(same, qt.astype(f32), -shift).astype(bf16)
            return 0

        lax.fori_loop(0, 2, half, 0)

    q_ref[...] = qaug[keep]
    attend(qaug.at[1 - keep], paug, pvt, out_ref, acc)


def attend(q_ref, paug, pvt, out_ref, acc):
    rows = q_ref.shape[0]
    slots = paug.shape[1]
    for t in range(rows // ROW_TILE):
        at = slice(t * ROW_TILE, (t + 1) * ROW_TILE)
        qt = q_ref[at, :]
        total = jnp.zeros((ROW_TILE, 128), f32)
        for j in range(slots // PT_TILE):
            cols = slice(j * PT_TILE, (j + 1) * PT_TILE)
            ex = jnp.exp2(dot(qt, paug[:, cols])).astype(bf16)
            total = total + dot(ex, pvt[cols, :])
        acc[at, :] = total

    sums = acc[...].reshape(2, GROUPS, 3, 8, 128)
    turned = pltpu.roll(acc[rows // 2 :, :], 64, 1).reshape(GROUPS, 3, 8, 128)
    lane = lanes((GROUPS, 8, 128))
    parts = [jnp.where(lane < 64, sums[0, :, q], turned[:, q]) for q in range(3)]
    extra = jnp.zeros((GROUPS, 8, 128), f32)
    for e in range(2):
        for q in range(3):
            extra = jnp.where(lane == 64 + 3 * e + q, sums[e, :, q], extra)
    out_ref[...] = jnp.concatenate(parts + [extra], axis=1).astype(bf16)

    shifts = -q_ref[...].astype(f32)
    at = lanes(shifts.shape)
    shifted = jnp.max(jnp.where((at >= 64) & (at < 67), jnp.abs(shifts), 0.0)) > 0.0

    @pl.when(shifted)
    def _():
        tiles = shifts.reshape(2, GROUPS, 3, 8, 128)
        more = extra
        for e in range(2):
            for q in range(3):
                for k in range(3):
                    one = tiles[e, :, q, :, 64 + k : 65 + k]
                    more = jnp.where(lane == 72 + 8 * k + 3 * e + q, one, more)
        out_ref[...] = jnp.concatenate(parts + [more], axis=1).astype(bf16)


def encode(pos, par, pn, normed, pack_own, pack_oth, small, paug, pvt):
    slots = paug.shape[1]
    rows = normed.shape[0] * HEADS // 2
    return pl.pallas_call(
        encode_kernel,
        out_shape=(shape((GROUPS, 32, 128)), shape((rows, 128))),
        in_specs=[smem()] * 3 + [vmem()] * 6,
        out_specs=(vmem(), vmem()),
        scratch_shapes=[
            pltpu.VMEM((2, 2, GROUPS, 3, 8, 128), f32),
            pltpu.VMEM((2, rows, 128), bf16),
            pltpu.VMEM((rows, 128), f32),
        ],
        compiler_params=params(),
        cost_estimate=cost(rows * slots * 1024, 6 << 20, rows * slots),
        name="encode",
    )(pos, par, pn, normed, pack_own, pack_oth, small, paug, pvt)


def encode_rest(queries, paug, pvt):
    rows, slots = queries.shape[0], paug.shape[1]
    return pl.pallas_call(
        attend,
        out_shape=shape((GROUPS, 32, 128)),
        in_specs=[vmem()] * 3,
        out_specs=vmem(),
        scratch_shapes=[pltpu.VMEM((rows, 128), f32)],
        compiler_params=params(),
        cost_estimate=cost(rows * slots * 1024, 6 << 20, rows * slots),
        name="encode_rest",
    )(queries, paug, pvt)


def pair_kernel(x_ref, y_ref, out_ref):
    xs = [x_ref[...].astype(f32), y_ref[...].astype(f32)]
    exts = [x[:, 24:32, :] for x in xs]
    lane = lanes(exts[0].shape)
    inside = (lane >= 72) & (lane < 96)
    flag = jnp.max(jnp.where(inside, jnp.maximum(jnp.abs(exts[0]), jnp.abs(exts[1])), 0.0))
    out_ref[...] = (xs[0] + xs[1]).astype(bf16)

    @pl.when(flag > 0.0)
    def _():
        shifts = [pltpu.roll(e, 128 - 8, 2) + pltpu.roll(e, 128 - 16, 2) + pltpu.roll(e, 128 - 24, 2) for e in exts]
        top = jnp.maximum(shifts[0], shifts[1])
        total = jnp.zeros(lane.shape, f32)
        parts = [jnp.zeros(lane.shape, f32) for _ in range(3)]
        here = (lane >= 64) & (lane < 70)
        for x, e, s in zip(xs, exts, shifts):
            wt = jnp.where(here, jnp.exp2(s - top), 0.0)
            total = total + e * wt
            for q in range(3):
                fac = jnp.where(lane < 64, wt[:, :, 64 + q : 65 + q], wt[:, :, 67 + q : 68 + q])
                parts[q] = parts[q] + x[:, q * 8 : (q + 1) * 8, :] * fac
        for k, part in enumerate(split3(jnp.where(here, top, 0.0))):
            total = total + pltpu.roll(part, 8 * (k + 1), 2)
        out_ref[...] = jnp.concatenate(parts + [total], axis=1).astype(bf16)


def pair(x, y):
    return pl.pallas_call(
        pair_kernel,
        out_shape=shape(x.shape),
        in_specs=[vmem()] * 2,
        out_specs=vmem(),
        compiler_params=params(),
        cost_estimate=cost(0, 1 << 20),
        name="pair",
    )(x, y)


def merge_kernel(x_ref, out_ref, both):
    x = x_ref[...].astype(f32)
    ext = x[:, 24:32, :]
    lane = lanes(ext.shape)
    flag = jnp.max(jnp.where((lane >= 72) & (lane < 96), jnp.abs(ext), 0.0))
    both[...] = jnp.sum(x, axis=0)

    @pl.when(flag > 0.0)
    def _():
        shift = pltpu.roll(ext, 128 - 8, 2) + pltpu.roll(ext, 128 - 16, 2) + pltpu.roll(ext, 128 - 24, 2)
        wt = jnp.exp2(shift - jnp.max(shift, axis=0, keepdims=True))
        wt = jnp.where((lane >= 64) & (lane < 70), wt, 0.0)
        both[24:32, :] = jnp.sum(ext * wt, axis=0)
        for q in range(3):
            fac = jnp.where(lane < 64, wt[:, :, 64 + q : 65 + q], wt[:, :, 67 + q : 68 + q])
            both[q * 8 : (q + 1) * 8, :] = jnp.sum(x[:, q * 8 : (q + 1) * 8, :] * fac, axis=0)

    low = lanes((8, 128)) < 64
    parts = []
    for q in range(3):
        tot = jnp.where(low, both[24:32, 64 + q : 65 + q], both[24:32, 67 + q : 68 + q])
        parts.append(both[q * 8 : (q + 1) * 8, :] / tot)
    mean = jnp.concatenate(parts, axis=0).astype(bf16)
    for k in range(out_ref.shape[0]):
        out_ref[k] = mean


def merge(parts, copies):
    return pl.pallas_call(
        merge_kernel,
        out_shape=shape((copies, 24, 128)),
        in_specs=[vmem()],
        out_specs=vmem(),
        scratch_shapes=[pltpu.VMEM((32, 128), f32)],
        compiler_params=params(),
        cost_estimate=cost(0, 1 << 20),
        name="merge",
    )(parts)


def latent_kernel(
    pos_ref, g_own, g_oth, pack_own, pack_oth, small,
    wl_own, wl_oth, up_own, up_oth, down_own, down_oth,
    at_ref, b_ref,
    enc, mix, wbuf, sem,
):
    rows = mix.shape[0]
    head = pos_ref[0]
    copies = {}
    for i in (2, 3, 1, 4, 5, 6):
        for k, (src, at) in enumerate(((wl_own, head), (wl_oth, 1 - head))):
            dst = wbuf.at[i - 1, pl.ds(pl.multiple_of(at * HALF, HALF), HALF)]
            copies[i, k] = pltpu.make_async_copy(src.at[i], dst, sem.at[i - 1, k])
            copies[i, k].start()
    for k, (g, pack) in enumerate(((g_own, pack_own), (g_oth, pack_oth))):
        mean = g[...].astype(f32).reshape(GROUPS, 2, 3, 8, 128)
        for p in range(PAIRS):
            cols = slice(p * 128, (p + 1) * 128)
            part = mean[:, p // 3, p % 3].reshape(rows, 128).astype(bf16)
            val = dot(part, block_diag(small[VAL : VAL + 64, cols]))
            enc[k * rows : (k + 1) * rows, cols] = (pack[HALF:, cols].astype(f32) + val).astype(bf16)
    block_in = norm(enc[...].astype(f32)).astype(bf16)

    def proj(x, i):
        for k in range(2):
            copies[i, k].wait()
        return dot(x, wbuf[i - 1])

    keys = proj(block_in, 2).astype(bf16)
    vals = proj(block_in, 3).astype(bf16)
    query = proj(block_in[:rows], 1).astype(bf16)
    ones = jnp.ones((2 * rows, 128), bf16)
    low = lanes((rows, 128)) < 64
    zero = jnp.zeros((rows, 128), bf16)
    for p in range(PAIRS):
        cols = slice(p * 128, (p + 1) * 128)
        qp = query[:, cols]
        both = jnp.concatenate([jnp.where(low, qp, zero), jnp.where(low, zero, qp)], axis=0)
        sc = dot(both, keys[:, cols], NT) * LOG2_SCALE
        ex = jnp.exp2(sc - jnp.max(sc, axis=-1, keepdims=True)).astype(bf16)
        res = dot(ex, jnp.concatenate([vals[:, cols], ones], axis=1))
        res = res[:, :128] / res[:, 128:]
        mix[:, cols] = jnp.where(low, res[:rows], res[rows:]).astype(bf16)
    latent2 = enc[:rows].astype(f32) + proj(mix[...], 4)
    mlp_in = norm(latent2).astype(bf16)
    hidden = []
    for up in (up_own, up_oth):
        x = dot(mlp_in, up[...])
        hid = 0.5 * x * (1.0 + jnp.tanh(math.sqrt(2.0 / math.pi) * (x + 0.044715 * (x * x * x))))
        hidden.append(hid.astype(bf16))
    latents_out = (latent2 + dot(hidden[0], down_own[...]) + dot(hidden[1], down_oth[...])).astype(bf16)
    dec_in = norm(latents_out.astype(f32)).astype(bf16)
    dkeys = proj(dec_in, 5).astype(bf16)
    for p in range(PAIRS):
        cols = slice(p * 128, (p + 1) * 128)
        at_ref[cols, :] = (dot(block_diag(small[QUERY : QUERY + 64, cols]), dkeys[:, cols], NT) * LOG2_SCALE).astype(bf16)
    dvals = proj(dec_in, 6).astype(bf16)
    classes = small[CLASS : CLASS + 16, :]
    lane = lanes(classes.shape)
    none = jnp.zeros_like(classes)
    blocks = [jnp.where((lane >= 64 * h) & (lane < 64 * h + 64), classes, none) for h in range(16)]
    b_ref[...] = dot(dvals, jnp.concatenate(blocks, axis=0), NT).astype(bf16)


def latent_block(pos, g_own, g_oth, pack_own, pack_oth, small, weights):
    rows = pack_own.shape[0] - HALF
    return pl.pallas_call(
        latent_kernel,
        out_shape=(shape((WIDTH, rows)), shape((rows, 256))),
        in_specs=[smem()] + [vmem()] * 5 + [anywhere()] * 2 + [vmem()] * 4,
        out_specs=(vmem(), vmem()),
        scratch_shapes=[
            pltpu.VMEM((2 * rows, WIDTH), bf16),
            pltpu.VMEM((rows, WIDTH), bf16),
            pltpu.VMEM((6, WIDTH, WIDTH), bf16),
            pltpu.SemaphoreType.DMA((6, 2)),
        ],
        compiler_params=params(),
        cost_estimate=cost(6 << 30, 20 << 20, 3 << 20),
        name="latent_block",
    )(pos, g_own, g_oth, pack_own, pack_oth, small, *weights)


DEC_TILE = 2048


def decode_kernel(pos_ref, pn_ref, pts_ref, at_own, at_oth, b_own, b_oth, out_ref, pt, amat, bmat):
    share = out_ref.shape[1]
    rows = b_own.shape[0]
    for i in range(share // 128):
        start = pl.multiple_of(pos_ref[0] * share + i * 128, 128)
        blk = pts_ref[:, pl.ds(start, 128)].astype(f32)
        full = jnp.concatenate([blk, jnp.zeros((64, 128), f32)], axis=0)
        pt[i * 128 : (i + 1) * 128, :] = full.T.astype(bf16)
    sub = lax.broadcasted_iota(jnp.int32, (64, 2 * rows), 0)
    lane = lanes((rows, 128))
    worst = jnp.zeros((1, rows), f32)
    for h in range(HEADS):
        amat[h, 64:128, :] = jnp.where((sub >= 3 * h) & (sub < 3 * h + 3), 1.0, 0.0).astype(bf16)
        for k, (a, b) in enumerate(((at_own, b_own), (at_oth, b_oth))):
            part = a[h * 64 : (h + 1) * 64, :]
            amat[h, 0:64, k * rows : (k + 1) * rows] = part
            part = part.astype(f32)
            worst = jnp.maximum(worst, jnp.sum(part * part, axis=0, keepdims=True))
            g = h // 8
            own = (lane >= 16 * (h % 8)) & (lane < 16 * (h % 8) + 16)
            vals = b[:, g * 128 : (g + 1) * 128]
            bmat[h, k * rows : (k + 1) * rows, 0:128] = jnp.where(own, vals, jnp.zeros_like(vals))
            bmat[h, k * rows : (k + 1) * rows, 128:256] = jnp.ones((rows, 128), bf16)
    lane = lanes((DEC_TILE, 128))

    @pl.when(jnp.max(worst) * pn_ref[0] > SAFE * SAFE)
    def _():
        def block(j, _):
            at = pl.ds(pl.multiple_of(j * DEC_TILE, DEC_TILE), DEC_TILE)
            pts = pt[at, :]
            new = pts.astype(f32)
            for h in range(HEADS):
                top = jnp.max(dot(pts, amat[h]), axis=1, keepdims=True)
                for k, part in enumerate(split3(top)):
                    new = jnp.where(lane == 64 + 3 * h + k, -part, new)
            pt[at, :] = new.astype(bf16)
            return 0

        lax.fori_loop(0, share // DEC_TILE, block, 0)

    def block(j, _):
        at = pl.ds(pl.multiple_of(j * DEC_TILE, DEC_TILE), DEC_TILE)
        pts = pt[at, :]
        total = jnp.zeros((DEC_TILE, 128), f32)
        coming = dot(pts, amat[0])
        for h in range(HEADS):
            sc = coming
            if h + 1 < HEADS:
                coming = dot(pts, amat[h + 1])
            res = dot(jnp.exp2(sc).astype(bf16), bmat[h])
            total = total + res[:, :128] / res[:, 128:]
        for turn in (64, 32, 16):
            total = total + pltpu.roll(total, turn, 1)
        out_ref[:, at] = total.T[0:16, :]
        return 0

    lax.fori_loop(0, share // DEC_TILE, block, 0)


def decode(pos, pn, points, at_own, at_oth, b_own, b_oth):
    rows = b_own.shape[0]
    share = points.shape[1] // 2
    return pl.pallas_call(
        decode_kernel,
        out_shape=shape((16, share), f32),
        in_specs=[smem(), smem()] + [vmem()] * 5,
        out_specs=vmem(),
        scratch_shapes=[
            pltpu.VMEM((share, 128), bf16),
            pltpu.VMEM((HEADS, 128, 2 * rows), bf16),
            pltpu.VMEM((HEADS, 2 * rows, 256), bf16),
        ],
        compiler_params=params(),
        cost_estimate=cost(3 << 32, 8 << 20, 12 << 20),
        name="decode",
    )(pos, pn, points, at_own, at_oth, b_own, b_oth)


PARITIES = [list(range(k, OWNERS, 2)) for k in range(2)]


def per_device(
    points, counts, latents_init, enc_key_w, enc_val_w, lat_weights, up_w, down_w, query_w, class_w
):
    swap = [(0, 1), (1, 0)]

    def other(x):
        return lax.ppermute(x, "head", swap)

    pos = lax.axis_index("head").astype(jnp.int32).reshape(1)
    par = (lax.axis_index("pts") & 1).astype(jnp.int32).reshape(1)
    pos, par, lat_weights = lax.optimization_barrier((pos, par, lat_weights))
    pack_own = jnp.concatenate([lat_weights[0], latents_init], axis=0)
    pack_oth = other(pack_own)
    small = jnp.concatenate([enc_key_w, enc_val_w, query_w, class_w.T], axis=0)
    paug, pvt, normed, pn = prepare(counts, points, pack_own, small)
    (pn, pack_oth), late = lax.optimization_barrier(((pn, pack_oth), (lat_weights, up_w, down_w)))
    wl_oth, up_oth, down_oth = [other(w) for w in late]
    away, queries = encode(pos, par, pn, normed, pack_own, pack_oth, small, paug, pvt)
    came = lax.ppermute(away, "pts", [(i, i ^ 1) for i in range(OWNERS)])
    part = pair(encode_rest(queries, paug, pvt), came)

    parts = lax.all_to_all(part, "pts", 0, 0, axis_index_groups=PARITIES)
    g_own = lax.all_to_all(merge(parts, OWNERS), "pts", 0, 0)
    g_oth = other(g_own)

    weights = (lat_weights, wl_oth, up_w, up_oth, down_w, down_oth)
    at_own, b_own = latent_block(pos, g_own, g_oth, pack_own, pack_oth, small, weights)
    return decode(pos, pn, points, at_own, other(at_own), b_own, other(b_own))


def solution(mesh):
    placed = (
        P(None, "pts"),
        P("pts"),
        P("head", None),
        P(),
        P(),
        P(None, "head", None),
        P(None, "head"),
        P("head", None),
        P(),
        P(),
    )
    return jax.shard_map(
        per_device, mesh=mesh, in_specs=placed, out_specs=P(None, ("pts", "head")), check_vma=False
    )
```

```python
import math

import jax
import jax.numpy as jnp
from jax import lax
from jax.experimental import pallas as pl
from jax.experimental.pallas import tpu as pltpu
from jax.sharding import PartitionSpec as P

HEADS = 12
HSIZE = 64
WIDTH = HEADS * HSIZE
PAIRS = HEADS // 2
HALF = WIDTH // 2
KEY, VAL, QUERY, CLASS = 0, 64, 128, 192
OWNERS = 64
GROUPS = 32
LOG2_SCALE = HSIZE ** -0.5 * math.log2(math.e)
SAFE = 64.0
DEAD = -1e30

f32 = jnp.float32
bf16 = jnp.bfloat16
NT = (((1,), (1,)), ((), ()))
NN = (((1,), (0,)), ((), ()))


def dot(a, b, dims=NN):
    return lax.dot_general(a, b, dims, preferred_element_type=f32)


def norm(v):
    mean = jnp.mean(v, axis=-1, keepdims=True)
    cent = v - mean
    var = jnp.mean(cent * cent, axis=-1, keepdims=True)
    return cent * lax.rsqrt(var + 1e-05)


def split3(v):
    hi = v.astype(bf16).astype(f32)
    mid = (v - hi).astype(bf16).astype(f32)
    lo = (v - hi - mid).astype(bf16).astype(f32)
    return hi, mid, lo


def lanes(shape):
    return lax.broadcasted_iota(jnp.int32, shape, len(shape) - 1)


def block_diag(pair):
    lane = lanes(pair.shape)
    zero = jnp.zeros_like(pair)
    return jnp.concatenate([jnp.where(lane < 64, pair, zero), jnp.where(lane >= 64, pair, zero)], axis=0)


def vmem():
    return pl.BlockSpec(memory_space=pltpu.VMEM)


def smem():
    return pl.BlockSpec(memory_space=pltpu.SMEM)


def anywhere():
    return pl.BlockSpec(memory_space=pl.ANY)


def shape(dims, dtype=bf16):
    return jax.ShapeDtypeStruct(dims, dtype)


def params(mib=28):
    return pltpu.CompilerParams(vmem_limit_bytes=mib << 20)


def cost(flops, size, exps=0):
    return pl.CostEstimate(flops=flops, bytes_accessed=size, transcendentals=exps)


def prepare_kernel(count_ref, pts_ref, pack_ref, before, paug, pvt, normed, pn_ref):
    slots = pts_ref.shape[1]
    count = count_ref[0]
    sub = lax.broadcasted_iota(jnp.int32, (64, slots), 0)
    col = lanes((64, slots))
    ext = jnp.where(sub < 3, 1.0, jnp.where((sub == 3) & (col >= count), DEAD, 0.0))
    paug[0:64, :] = pts_ref[...]
    paug[64:128, :] = ext.astype(bf16)
    for i in range(slots // 128):
        blk = pts_ref[:, i * 128 : (i + 1) * 128].astype(f32)
        full = jnp.concatenate([blk, jnp.ones((64, 128), f32)], axis=0)
        pvt[i * 128 : (i + 1) * 128, :] = full.T.astype(bf16)
    normed[...] = norm(pack_ref[HALF:, :].astype(f32)).astype(bf16)
    pall = pts_ref[...].astype(f32)
    pn_ref[0] = jnp.max(jnp.sum(pall * pall, axis=0, keepdims=True))


def prepare(count, points, pack, before):
    slots = points.shape[1]
    return pl.pallas_call(
        prepare_kernel,
        out_shape=(shape((128, slots)), shape((slots, 128)), shape((pack.shape[0] - HALF, WIDTH)), shape((1,), f32)),
        in_specs=[smem(), vmem(), vmem(), anywhere()],
        out_specs=(vmem(), vmem(), vmem(), smem()),
        compiler_params=params(),
        cost_estimate=cost(0, 6 << 20),
        name="prepare",
    )(count, points, pack, before)


ROW_TILE = 768
TOP_ROWS = 256
PT_TILE = 512


def encode_kernel(pos_ref, par_ref, pn_ref, normed, pack_own, pack_oth, small, paug, pvt, out_ref, q_ref, qf, qaug, acc):
    rows = qaug.shape[1]
    slots = paug.shape[1]
    keep = par_ref[0]

    lo, hi = normed[:, :HALF], normed[:, HALF:]
    first = pos_ref[0] == 0
    equery = dot(jnp.where(first, lo, hi), pack_own[:HALF, :]) + dot(jnp.where(first, hi, lo), pack_oth[:HALF, :])
    equery = equery.astype(bf16)
    lane8 = lanes((GROUPS, 8, 128))
    aug = jnp.where(lane8 == 67, 1.0, 0.0)
    for p in range(PAIRS):
        cols = slice(p * 128, (p + 1) * 128)
        x = dot(equery[:, cols], block_diag(small[KEY : KEY + 64, cols]), NT) * LOG2_SCALE
        x8 = x.reshape(GROUPS, 8, 128)
        y8 = pltpu.roll(x, 64, 1).reshape(GROUPS, 8, 128)
        s, q = p // 3, p % 3
        qf[s, 0, :, q] = jnp.where(lane8 < 64, x8, aug)
        qf[s, 1, :, q] = jnp.where(lane8 < 64, y8, aug)
    qall = qf[...].reshape(2 * rows, 128)
    qaug[...] = qall.astype(bf16).reshape(2, rows, 128)

    sub = lax.broadcasted_iota(jnp.int32, (128, 128), 0)
    sums = dot((qall * qall).astype(bf16), jnp.where(sub < 64, 1.0, 0.0).astype(bf16))
    shifted = jnp.max(sums) * pn_ref[0] > SAFE * SAFE

    @pl.when(shifted)
    def _():
        def tile(t, _):
            per = rows // TOP_ROWS
            at = pl.ds(pl.multiple_of(lax.rem(t, per) * TOP_ROWS, TOP_ROWS), TOP_ROWS)
            qt = qaug[t // per, at, :]

            def chunk(j, top):
                start = pl.multiple_of(j * PT_TILE, PT_TILE)
                sc = dot(qt, paug[:, pl.ds(start, PT_TILE)])
                return jnp.maximum(top, jnp.max(sc, axis=1, keepdims=True))

            top = lax.fori_loop(0, slots // PT_TILE, chunk, jnp.full((TOP_ROWS, 1), DEAD, f32))
            hi, mid, lo = split3(top)
            lane = lanes((TOP_ROWS, 128))
            shift = jnp.where(lane == 64, hi, jnp.where(lane == 65, mid, lo))
            same = (lane < 64) | (lane > 66)
            qaug[t // per, at, :] = jnp.where(same, qt.astype(f32), -shift).astype(bf16)
            return 0

        lax.fori_loop(0, 2 * rows // TOP_ROWS, tile, 0)

    q_ref[...] = qaug[keep]
    attend(qaug.at[1 - keep], paug, pvt, out_ref, acc)


def attend(q_ref, paug, pvt, out_ref, acc):
    rows = q_ref.shape[0]
    slots = paug.shape[1]

    def tile(t, _):
        at = pl.ds(pl.multiple_of(t * ROW_TILE, ROW_TILE), ROW_TILE)
        qt = q_ref[at, :]
        total = jnp.zeros((ROW_TILE, 128), f32)
        for j in range(slots // PT_TILE):
            cols = slice(j * PT_TILE, (j + 1) * PT_TILE)
            ex = jnp.exp2(dot(qt, paug[:, cols])).astype(bf16)
            total = total + dot(ex, pvt[cols, :])
        acc[at, :] = total
        return 0

    lax.fori_loop(0, rows // ROW_TILE, tile, 0)

    sums = acc[...].reshape(2, GROUPS, 3, 8, 128)
    turned = pltpu.roll(acc[rows // 2 :, :], 64, 1).reshape(GROUPS, 3, 8, 128)
    lane = lanes((GROUPS, 8, 128))
    parts = [jnp.where(lane < 64, sums[0, :, q], turned[:, q]) for q in range(3)]
    extra = jnp.zeros((GROUPS, 8, 128), f32)
    for e in range(2):
        for q in range(3):
            extra = jnp.where(lane == 64 + 3 * e + q, sums[e, :, q], extra)
    out_ref[...] = jnp.concatenate(parts + [extra], axis=1).astype(bf16)

    shifts = -q_ref[...].astype(f32)
    at = lanes(shifts.shape)
    shifted = jnp.max(jnp.where((at >= 64) & (at < 67), jnp.abs(shifts), 0.0)) > 0.0

    @pl.when(shifted)
    def _():
        tiles = shifts.reshape(2, GROUPS, 3, 8, 128)
        more = extra
        for e in range(2):
            for q in range(3):
                for k in range(3):
                    one = tiles[e, :, q, :, 64 + k : 65 + k]
                    more = jnp.where(lane == 72 + 8 * k + 3 * e + q, one, more)
        out_ref[...] = jnp.concatenate(parts + [more], axis=1).astype(bf16)


def encode(pos, par, pn, normed, pack_own, pack_oth, small, paug, pvt):
    slots = paug.shape[1]
    rows = normed.shape[0] * HEADS // 2
    return pl.pallas_call(
        encode_kernel,
        out_shape=(shape((GROUPS, 32, 128)), shape((rows, 128))),
        in_specs=[smem()] * 3 + [vmem()] * 6,
        out_specs=(vmem(), vmem()),
        scratch_shapes=[
            pltpu.VMEM((2, 2, GROUPS, 3, 8, 128), f32),
            pltpu.VMEM((2, rows, 128), bf16),
            pltpu.VMEM((rows, 128), f32),
        ],
        compiler_params=params(),
        cost_estimate=cost(rows * slots * 1024, 6 << 20, rows * slots),
        name="encode",
    )(pos, par, pn, normed, pack_own, pack_oth, small, paug, pvt)


def encode_rest(queries, paug, pvt):
    rows, slots = queries.shape[0], paug.shape[1]
    return pl.pallas_call(
        attend,
        out_shape=shape((GROUPS, 32, 128)),
        in_specs=[vmem()] * 3,
        out_specs=vmem(),
        scratch_shapes=[pltpu.VMEM((rows, 128), f32)],
        compiler_params=params(),
        cost_estimate=cost(rows * slots * 1024, 6 << 20, rows * slots),
        name="encode_rest",
    )(queries, paug, pvt)


def pair_kernel(x_ref, y_ref, out_ref):
    xs = [x_ref[...].astype(f32), y_ref[...].astype(f32)]
    exts = [x[:, 24:32, :] for x in xs]
    lane = lanes(exts[0].shape)
    inside = (lane >= 72) & (lane < 96)
    flag = jnp.max(jnp.where(inside, jnp.maximum(jnp.abs(exts[0]), jnp.abs(exts[1])), 0.0))
    out_ref[...] = (xs[0] + xs[1]).astype(bf16)

    @pl.when(flag > 0.0)
    def _():
        shifts = [pltpu.roll(e, 128 - 8, 2) + pltpu.roll(e, 128 - 16, 2) + pltpu.roll(e, 128 - 24, 2) for e in exts]
        top = jnp.maximum(shifts[0], shifts[1])
        total = jnp.zeros(lane.shape, f32)
        parts = [jnp.zeros(lane.shape, f32) for _ in range(3)]
        here = (lane >= 64) & (lane < 70)
        for x, e, s in zip(xs, exts, shifts):
            wt = jnp.where(here, jnp.exp2(s - top), 0.0)
            total = total + e * wt
            for q in range(3):
                fac = jnp.where(lane < 64, wt[:, :, 64 + q : 65 + q], wt[:, :, 67 + q : 68 + q])
                parts[q] = parts[q] + x[:, q * 8 : (q + 1) * 8, :] * fac
        for k, part in enumerate(split3(jnp.where(here, top, 0.0))):
            total = total + pltpu.roll(part, 8 * (k + 1), 2)
        out_ref[...] = jnp.concatenate(parts + [total], axis=1).astype(bf16)


def pair(x, y):
    return pl.pallas_call(
        pair_kernel,
        out_shape=shape(x.shape),
        in_specs=[vmem()] * 2,
        out_specs=vmem(),
        compiler_params=params(),
        cost_estimate=cost(0, 1 << 20),
        name="pair",
    )(x, y)


def merge_kernel(x_ref, out_ref, both):
    x = x_ref[...].astype(f32)
    ext = x[:, 24:32, :]
    lane = lanes(ext.shape)
    flag = jnp.max(jnp.where((lane >= 72) & (lane < 96), jnp.abs(ext), 0.0))
    both[...] = jnp.sum(x, axis=0)

    @pl.when(flag > 0.0)
    def _():
        shift = pltpu.roll(ext, 128 - 8, 2) + pltpu.roll(ext, 128 - 16, 2) + pltpu.roll(ext, 128 - 24, 2)
        wt = jnp.exp2(shift - jnp.max(shift, axis=0, keepdims=True))
        wt = jnp.where((lane >= 64) & (lane < 70), wt, 0.0)
        both[24:32, :] = jnp.sum(ext * wt, axis=0)
        for q in range(3):
            fac = jnp.where(lane < 64, wt[:, :, 64 + q : 65 + q], wt[:, :, 67 + q : 68 + q])
            both[q * 8 : (q + 1) * 8, :] = jnp.sum(x[:, q * 8 : (q + 1) * 8, :] * fac, axis=0)

    low = lanes((8, 128)) < 64
    parts = []
    for q in range(3):
        tot = jnp.where(low, both[24:32, 64 + q : 65 + q], both[24:32, 67 + q : 68 + q])
        parts.append(both[q * 8 : (q + 1) * 8, :] / tot)
    mean = jnp.concatenate(parts, axis=0).astype(bf16)
    for k in range(out_ref.shape[0]):
        out_ref[k] = mean


def merge(parts, copies):
    return pl.pallas_call(
        merge_kernel,
        out_shape=shape((copies, 24, 128)),
        in_specs=[vmem()],
        out_specs=vmem(),
        scratch_shapes=[pltpu.VMEM((32, 128), f32)],
        compiler_params=params(),
        cost_estimate=cost(0, 1 << 20),
        name="merge",
    )(parts)


def latent_kernel(
    pos_ref, g_own, g_oth, pack_own, pack_oth, small,
    wl_own, wl_oth, up_own, up_oth, down_own, down_oth,
    at_ref, b_ref,
    enc, mix, wbuf, sem,
):
    rows = mix.shape[0]
    head = pos_ref[0]
    copies = {}
    for i in (2, 3, 1, 4, 5, 6):
        for k, (src, at) in enumerate(((wl_own, head), (wl_oth, 1 - head))):
            dst = wbuf.at[i - 1, pl.ds(pl.multiple_of(at * HALF, HALF), HALF)]
            copies[i, k] = pltpu.make_async_copy(src.at[i], dst, sem.at[i - 1, k])
            copies[i, k].start()
    for k, (g, pack) in enumerate(((g_own, pack_own), (g_oth, pack_oth))):
        mean = g[...].astype(f32).reshape(GROUPS, 2, 3, 8, 128)
        for p in range(PAIRS):
            cols = slice(p * 128, (p + 1) * 128)
            part = mean[:, p // 3, p % 3].reshape(rows, 128).astype(bf16)
            val = dot(part, block_diag(small[VAL : VAL + 64, cols]))
            enc[k * rows : (k + 1) * rows, cols] = (pack[HALF:, cols].astype(f32) + val).astype(bf16)
    block_in = norm(enc[...].astype(f32)).astype(bf16)

    def proj(x, i):
        for k in range(2):
            copies[i, k].wait()
        return dot(x, wbuf[i - 1])

    keys = proj(block_in, 2).astype(bf16)
    vals = proj(block_in, 3).astype(bf16)
    query = proj(block_in[:rows], 1).astype(bf16)
    ones = jnp.ones((2 * rows, 128), bf16)
    low = lanes((rows, 128)) < 64
    zero = jnp.zeros((rows, 128), bf16)
    for p in range(PAIRS):
        cols = slice(p * 128, (p + 1) * 128)
        qp = query[:, cols]
        both = jnp.concatenate([jnp.where(low, qp, zero), jnp.where(low, zero, qp)], axis=0)
        sc = dot(both, keys[:, cols], NT) * LOG2_SCALE
        ex = jnp.exp2(sc - jnp.max(sc, axis=-1, keepdims=True)).astype(bf16)
        res = dot(ex, jnp.concatenate([vals[:, cols], ones], axis=1))
        res = res[:, :128] / res[:, 128:]
        mix[:, cols] = jnp.where(low, res[:rows], res[rows:]).astype(bf16)
    latent2 = enc[:rows].astype(f32) + proj(mix[...], 4)
    mlp_in = norm(latent2).astype(bf16)
    hidden = []
    for up in (up_own, up_oth):
        x = dot(mlp_in, up[...])
        hid = 0.5 * x * (1.0 + jnp.tanh(math.sqrt(2.0 / math.pi) * (x + 0.044715 * (x * x * x))))
        hidden.append(hid.astype(bf16))
    latents_out = (latent2 + dot(hidden[0], down_own[...]) + dot(hidden[1], down_oth[...])).astype(bf16)
    dec_in = norm(latents_out.astype(f32)).astype(bf16)
    dkeys = proj(dec_in, 5).astype(bf16)
    for p in range(PAIRS):
        cols = slice(p * 128, (p + 1) * 128)
        at_ref[cols, :] = (dot(block_diag(small[QUERY : QUERY + 64, cols]), dkeys[:, cols], NT) * LOG2_SCALE).astype(bf16)
    dvals = proj(dec_in, 6).astype(bf16)
    classes = small[CLASS : CLASS + 16, :]
    lane = lanes(classes.shape)
    none = jnp.zeros_like(classes)
    blocks = [jnp.where((lane >= 64 * h) & (lane < 64 * h + 64), classes, none) for h in range(16)]
    b_ref[...] = dot(dvals, jnp.concatenate(blocks, axis=0), NT).astype(bf16)


def latent_block(pos, g_own, g_oth, pack_own, pack_oth, small, weights):
    rows = pack_own.shape[0] - HALF
    return pl.pallas_call(
        latent_kernel,
        out_shape=(shape((WIDTH, rows)), shape((rows, 256))),
        in_specs=[smem()] + [vmem()] * 5 + [anywhere()] * 2 + [vmem()] * 4,
        out_specs=(vmem(), vmem()),
        scratch_shapes=[
            pltpu.VMEM((2 * rows, WIDTH), bf16),
            pltpu.VMEM((rows, WIDTH), bf16),
            pltpu.VMEM((6, WIDTH, WIDTH), bf16),
            pltpu.SemaphoreType.DMA((6, 2)),
        ],
        compiler_params=params(),
        cost_estimate=cost(6 << 30, 20 << 20, 3 << 20),
        name="latent_block",
    )(pos, g_own, g_oth, pack_own, pack_oth, small, *weights)


DEC_TILE = 1024
TOP_TILE = 128


def decode_kernel(pos_ref, pn_ref, pts_ref, at_own, at_oth, b_own, b_oth, out_ref, pt, amat, bmat):
    share = out_ref.shape[1]
    rows = b_own.shape[0]
    for i in range(share // 128):
        start = pl.multiple_of(pos_ref[0] * share + i * 128, 128)
        blk = pts_ref[:, pl.ds(start, 128)].astype(f32)
        full = jnp.concatenate([blk, jnp.zeros((64, 128), f32)], axis=0)
        pt[i * 128 : (i + 1) * 128, :] = full.T.astype(bf16)
    sub = lax.broadcasted_iota(jnp.int32, (64, 2 * rows), 0)
    lane = lanes((rows, 128))
    worst = jnp.zeros((1, rows), f32)
    for h in range(HEADS):
        amat[h, 64:128, :] = jnp.where((sub >= 3 * h) & (sub < 3 * h + 3), 1.0, 0.0).astype(bf16)
        for k, (a, b) in enumerate(((at_own, b_own), (at_oth, b_oth))):
            part = a[h * 64 : (h + 1) * 64, :]
            amat[h, 0:64, k * rows : (k + 1) * rows] = part
            part = part.astype(f32)
            worst = jnp.maximum(worst, jnp.sum(part * part, axis=0, keepdims=True))
            g = h // 8
            own = (lane >= 16 * (h % 8)) & (lane < 16 * (h % 8) + 16)
            vals = b[:, g * 128 : (g + 1) * 128]
            bmat[h, k * rows : (k + 1) * rows, 0:128] = jnp.where(own, vals, jnp.zeros_like(vals))
            bmat[h, k * rows : (k + 1) * rows, 128:256] = jnp.ones((rows, 128), bf16)

    @pl.when(jnp.max(worst) * pn_ref[0] > SAFE * SAFE)
    def _():
        def tops(j, _):
            at = pl.ds(pl.multiple_of(j * TOP_TILE, TOP_TILE), TOP_TILE)
            pts = pt[at, :]
            new = pts.astype(f32)
            few = lanes((TOP_TILE, 128))
            for h in range(HEADS):
                top = jnp.max(dot(pts, amat[h]), axis=1, keepdims=True)
                for k, part in enumerate(split3(top)):
                    new = jnp.where(few == 64 + 3 * h + k, -part, new)
            pt[at, :] = new.astype(bf16)
            return 0

        lax.fori_loop(0, share // TOP_TILE, tops, 0)

    def block(j, _):
        at = pl.ds(pl.multiple_of(j * DEC_TILE, DEC_TILE), DEC_TILE)
        pts = pt[at, :]
        total = jnp.zeros((DEC_TILE, 128), f32)
        coming = dot(pts, amat[0])
        for h in range(HEADS):
            sc = coming
            if h + 1 < HEADS:
                coming = dot(pts, amat[h + 1])
            res = dot(jnp.exp2(sc).astype(bf16), bmat[h])
            total = total + res[:, :128] / res[:, 128:]
        for turn in (64, 32, 16):
            total = total + pltpu.roll(total, turn, 1)
        out_ref[:, at] = total.T[0:16, :]
        return 0

    lax.fori_loop(0, share // DEC_TILE, block, 0)


def decode(pos, pn, points, at_own, at_oth, b_own, b_oth):
    rows = b_own.shape[0]
    share = points.shape[1] // 2
    return pl.pallas_call(
        decode_kernel,
        out_shape=shape((16, share), f32),
        in_specs=[smem(), smem()] + [vmem()] * 5,
        out_specs=vmem(),
        scratch_shapes=[
            pltpu.VMEM((share, 128), bf16),
            pltpu.VMEM((HEADS, 128, 2 * rows), bf16),
            pltpu.VMEM((HEADS, 2 * rows, 256), bf16),
        ],
        compiler_params=params(),
        cost_estimate=cost(3 << 32, 8 << 20, 12 << 20),
        name="decode",
    )(pos, pn, points, at_own, at_oth, b_own, b_oth)


PARITIES = [list(range(k, OWNERS, 2)) for k in range(2)]


def per_device(
    points, counts, latents_init, enc_key_w, enc_val_w, lat_weights, up_w, down_w, query_w, class_w
):
    swap = [(0, 1), (1, 0)]

    def other(x):
        return lax.ppermute(x, "head", swap)

    pos = lax.axis_index("head").astype(jnp.int32).reshape(1)
    par = (lax.axis_index("pts") & 1).astype(jnp.int32).reshape(1)
    pos, par, lat_weights = lax.optimization_barrier((pos, par, lat_weights))
    pack_own = jnp.concatenate([lat_weights[0], latents_init], axis=0)
    pack_oth = other(pack_own)
    small = jnp.concatenate([enc_key_w, enc_val_w, query_w, class_w.T], axis=0)
    paug, pvt, normed, pn = prepare(counts, points, pack_own, small)
    (pn, pack_oth), late = lax.optimization_barrier(((pn, pack_oth), (lat_weights, up_w, down_w)))
    wl_oth, up_oth, down_oth = [other(w) for w in late]
    away, queries = encode(pos, par, pn, normed, pack_own, pack_oth, small, paug, pvt)
    came = lax.ppermute(away, "pts", [(i, i ^ 1) for i in range(OWNERS)])
    part = pair(encode_rest(queries, paug, pvt), came)

    parts = lax.all_to_all(part, "pts", 0, 0, axis_index_groups=PARITIES)
    g_own = lax.all_to_all(merge(parts, OWNERS), "pts", 0, 0)
    g_oth = other(g_own)

    weights = (lat_weights, wl_oth, up_w, up_oth, down_w, down_oth)
    at_own, b_own = latent_block(pos, g_own, g_oth, pack_own, pack_oth, small, weights)
    return decode(pos, pn, points, at_own, other(at_own), b_own, other(b_own))


def solution(mesh):
    placed = (
        P(None, "pts"),
        P("pts"),
        P("head", None),
        P(),
        P(),
        P(None, "head", None),
        P(None, "head"),
        P("head", None),
        P(),
        P(),
    )
    return jax.shard_map(
        per_device, mesh=mesh, in_specs=placed, out_specs=P(None, ("pts", "head")), check_vma=False
    )
```

```python
import math

import jax
import jax.numpy as jnp
from jax import lax
from jax.experimental import pallas as pl
from jax.experimental.pallas import tpu as pltpu
from jax.sharding import PartitionSpec as P

HEADS = 12
HSIZE = 64
WIDTH = HEADS * HSIZE
PAIRS = HEADS // 2
HALF = WIDTH // 2
KEY, VAL, QUERY, CLASS = 0, 64, 128, 192
OWNERS = 64
GROUPS = 32
LOG2_SCALE = HSIZE ** -0.5 * math.log2(math.e)
SAFE = 64.0
DEAD = -1e30

f32 = jnp.float32
bf16 = jnp.bfloat16
NT = (((1,), (1,)), ((), ()))
NN = (((1,), (0,)), ((), ()))


def dot(a, b, dims=NN):
    return lax.dot_general(a, b, dims, preferred_element_type=f32)


def norm(v):
    mean = jnp.mean(v, axis=-1, keepdims=True)
    cent = v - mean
    var = jnp.mean(cent * cent, axis=-1, keepdims=True)
    return cent * lax.rsqrt(var + 1e-05)


def split3(v):
    hi = v.astype(bf16).astype(f32)
    mid = (v - hi).astype(bf16).astype(f32)
    lo = (v - hi - mid).astype(bf16).astype(f32)
    return hi, mid, lo


def lanes(shape):
    return lax.broadcasted_iota(jnp.int32, shape, len(shape) - 1)


def block_diag(pair):
    lane = lanes(pair.shape)
    zero = jnp.zeros_like(pair)
    return jnp.concatenate([jnp.where(lane < 64, pair, zero), jnp.where(lane >= 64, pair, zero)], axis=0)


def vmem():
    return pl.BlockSpec(memory_space=pltpu.VMEM)


def smem():
    return pl.BlockSpec(memory_space=pltpu.SMEM)


def anywhere():
    return pl.BlockSpec(memory_space=pl.ANY)


def shape(dims, dtype=bf16):
    return jax.ShapeDtypeStruct(dims, dtype)


def params(mib=28):
    return pltpu.CompilerParams(vmem_limit_bytes=mib << 20)


def cost(flops, size, exps=0):
    return pl.CostEstimate(flops=flops, bytes_accessed=size, transcendentals=exps)


def prepare_kernel(count_ref, pts_ref, pack_ref, before, paug, pvt, normed, pn_ref):
    slots = pts_ref.shape[1]
    count = count_ref[0]
    sub = lax.broadcasted_iota(jnp.int32, (64, slots), 0)
    col = lanes((64, slots))
    ext = jnp.where(sub < 3, 1.0, jnp.where((sub == 3) & (col >= count), DEAD, 0.0))
    paug[0:64, :] = pts_ref[...]
    paug[64:128, :] = ext.astype(bf16)
    for i in range(slots // 128):
        blk = pts_ref[:, i * 128 : (i + 1) * 128].astype(f32)
        full = jnp.concatenate([blk, jnp.ones((64, 128), f32)], axis=0)
        pvt[i * 128 : (i + 1) * 128, :] = full.T.astype(bf16)
    normed[...] = norm(pack_ref[HALF:, :].astype(f32)).astype(bf16)
    pall = pts_ref[...].astype(f32)
    pn_ref[0] = jnp.max(jnp.sum(pall * pall, axis=0, keepdims=True))


def prepare(count, points, pack, before):
    slots = points.shape[1]
    return pl.pallas_call(
        prepare_kernel,
        out_shape=(shape((128, slots)), shape((slots, 128)), shape((pack.shape[0] - HALF, WIDTH)), shape((1,), f32)),
        in_specs=[smem(), vmem(), vmem(), anywhere()],
        out_specs=(vmem(), vmem(), vmem(), smem()),
        compiler_params=params(),
        cost_estimate=cost(0, 6 << 20),
        name="prepare",
    )(count, points, pack, before)


PT_TURN = 4 * 512
TOP_ROWS = 256
PT_TILE = 512


def encode_kernel(pos_ref, par_ref, pn_ref, normed, pack_own, pack_oth, small, paug, pvt, out_ref, q_ref, qf, qaug, acc):
    rows = qaug.shape[1]
    slots = paug.shape[1]
    keep = par_ref[0]

    lo, hi = normed[:, :HALF], normed[:, HALF:]
    first = pos_ref[0] == 0
    equery = dot(jnp.where(first, lo, hi), pack_own[:HALF, :]) + dot(jnp.where(first, hi, lo), pack_oth[:HALF, :])
    equery = equery.astype(bf16)
    lane8 = lanes((GROUPS, 8, 128))
    aug = jnp.where(lane8 == 67, 1.0, 0.0)
    for p in range(PAIRS):
        cols = slice(p * 128, (p + 1) * 128)
        x = dot(equery[:, cols], block_diag(small[KEY : KEY + 64, cols]), NT) * LOG2_SCALE
        x8 = x.reshape(GROUPS, 8, 128)
        y8 = pltpu.roll(x, 64, 1).reshape(GROUPS, 8, 128)
        s, q = p // 3, p % 3
        qf[s, 0, :, q] = jnp.where(lane8 < 64, x8, aug)
        qf[s, 1, :, q] = jnp.where(lane8 < 64, y8, aug)
    qall = qf[...].reshape(2 * rows, 128)
    qaug[...] = qall.astype(bf16).reshape(2, rows, 128)

    sub = lax.broadcasted_iota(jnp.int32, (128, 128), 0)
    sums = dot((qall * qall).astype(bf16), jnp.where(sub < 64, 1.0, 0.0).astype(bf16))
    shifted = jnp.max(sums) * pn_ref[0] > SAFE * SAFE

    @pl.when(shifted)
    def _():
        def tile(t, _):
            per = rows // TOP_ROWS
            at = pl.ds(pl.multiple_of(lax.rem(t, per) * TOP_ROWS, TOP_ROWS), TOP_ROWS)
            qt = qaug[t // per, at, :]

            def chunk(j, top):
                start = pl.multiple_of(j * PT_TILE, PT_TILE)
                sc = dot(qt, paug[:, pl.ds(start, PT_TILE)])
                return jnp.maximum(top, jnp.max(sc, axis=1, keepdims=True))

            top = lax.fori_loop(0, slots // PT_TILE, chunk, jnp.full((TOP_ROWS, 1), DEAD, f32))
            hi, mid, lo = split3(top)
            lane = lanes((TOP_ROWS, 128))
            shift = jnp.where(lane == 64, hi, jnp.where(lane == 65, mid, lo))
            same = (lane < 64) | (lane > 66)
            qaug[t // per, at, :] = jnp.where(same, qt.astype(f32), -shift).astype(bf16)
            return 0

        lax.fori_loop(0, 2 * rows // TOP_ROWS, tile, 0)

    q_ref[...] = qaug[keep]
    attend(qaug.at[1 - keep], paug, pvt, out_ref, acc)


def attend(q_ref, paug, pvt, out_ref, acc):
    rows = q_ref.shape[0]
    slots = paug.shape[1]
    qt = q_ref[...]
    acc[...] = jnp.zeros(acc.shape, f32)

    def turn(t, _):
        total = acc[...]
        for j in range(PT_TURN // PT_TILE):
            cols = pl.ds(pl.multiple_of(t * PT_TURN + j * PT_TILE, PT_TILE), PT_TILE)
            ex = jnp.exp2(dot(qt, paug[:, cols])).astype(bf16)
            total = total + dot(ex, pvt[cols, :])
        acc[...] = total
        return 0

    lax.fori_loop(0, slots // PT_TURN, turn, 0)

    sums = acc[...].reshape(2, GROUPS, 3, 8, 128)
    turned = pltpu.roll(acc[rows // 2 :, :], 64, 1).reshape(GROUPS, 3, 8, 128)
    lane = lanes((GROUPS, 8, 128))
    parts = [jnp.where(lane < 64, sums[0, :, q], turned[:, q]) for q in range(3)]
    extra = jnp.zeros((GROUPS, 8, 128), f32)
    for e in range(2):
        for q in range(3):
            extra = jnp.where(lane == 64 + 3 * e + q, sums[e, :, q], extra)
    out_ref[...] = jnp.concatenate(parts + [extra], axis=1).astype(bf16)

    shifts = -q_ref[...].astype(f32)
    at = lanes(shifts.shape)
    shifted = jnp.max(jnp.where((at >= 64) & (at < 67), jnp.abs(shifts), 0.0)) > 0.0

    @pl.when(shifted)
    def _():
        tiles = shifts.reshape(2, GROUPS, 3, 8, 128)
        more = extra
        for e in range(2):
            for q in range(3):
                for k in range(3):
                    one = tiles[e, :, q, :, 64 + k : 65 + k]
                    more = jnp.where(lane == 72 + 8 * k + 3 * e + q, one, more)
        out_ref[...] = jnp.concatenate(parts + [more], axis=1).astype(bf16)


def encode(pos, par, pn, normed, pack_own, pack_oth, small, paug, pvt):
    slots = paug.shape[1]
    rows = normed.shape[0] * HEADS // 2
    return pl.pallas_call(
        encode_kernel,
        out_shape=(shape((GROUPS, 32, 128)), shape((rows, 128))),
        in_specs=[smem()] * 3 + [vmem()] * 6,
        out_specs=(vmem(), vmem()),
        scratch_shapes=[
            pltpu.VMEM((2, 2, GROUPS, 3, 8, 128), f32),
            pltpu.VMEM((2, rows, 128), bf16),
            pltpu.VMEM((rows, 128), f32),
        ],
        compiler_params=params(),
        cost_estimate=cost(rows * slots * 1024, 6 << 20, rows * slots),
        name="encode",
    )(pos, par, pn, normed, pack_own, pack_oth, small, paug, pvt)


def encode_rest(queries, paug, pvt):
    rows, slots = queries.shape[0], paug.shape[1]
    return pl.pallas_call(
        attend,
        out_shape=shape((GROUPS, 32, 128)),
        in_specs=[vmem()] * 3,
        out_specs=vmem(),
        scratch_shapes=[pltpu.VMEM((rows, 128), f32)],
        compiler_params=params(),
        cost_estimate=cost(rows * slots * 1024, 6 << 20, rows * slots),
        name="encode_rest",
    )(queries, paug, pvt)


def pair_kernel(x_ref, y_ref, out_ref):
    xs = [x_ref[...].astype(f32), y_ref[...].astype(f32)]
    exts = [x[:, 24:32, :] for x in xs]
    lane = lanes(exts[0].shape)
    inside = (lane >= 72) & (lane < 96)
    flag = jnp.max(jnp.where(inside, jnp.maximum(jnp.abs(exts[0]), jnp.abs(exts[1])), 0.0))
    out_ref[...] = (xs[0] + xs[1]).astype(bf16)

    @pl.when(flag > 0.0)
    def _():
        shifts = [pltpu.roll(e, 128 - 8, 2) + pltpu.roll(e, 128 - 16, 2) + pltpu.roll(e, 128 - 24, 2) for e in exts]
        top = jnp.maximum(shifts[0], shifts[1])
        total = jnp.zeros(lane.shape, f32)
        parts = [jnp.zeros(lane.shape, f32) for _ in range(3)]
        here = (lane >= 64) & (lane < 70)
        for x, e, s in zip(xs, exts, shifts):
            wt = jnp.where(here, jnp.exp2(s - top), 0.0)
            total = total + e * wt
            for q in range(3):
                fac = jnp.where(lane < 64, wt[:, :, 64 + q : 65 + q], wt[:, :, 67 + q : 68 + q])
                parts[q] = parts[q] + x[:, q * 8 : (q + 1) * 8, :] * fac
        for k, part in enumerate(split3(jnp.where(here, top, 0.0))):
            total = total + pltpu.roll(part, 8 * (k + 1), 2)
        out_ref[...] = jnp.concatenate(parts + [total], axis=1).astype(bf16)


def pair(x, y):
    return pl.pallas_call(
        pair_kernel,
        out_shape=shape(x.shape),
        in_specs=[vmem()] * 2,
        out_specs=vmem(),
        compiler_params=params(),
        cost_estimate=cost(0, 1 << 20),
        name="pair",
    )(x, y)


def merge_kernel(x_ref, out_ref, both):
    x = x_ref[...].astype(f32)
    ext = x[:, 24:32, :]
    lane = lanes(ext.shape)
    flag = jnp.max(jnp.where((lane >= 72) & (lane < 96), jnp.abs(ext), 0.0))
    both[...] = jnp.sum(x, axis=0)

    @pl.when(flag > 0.0)
    def _():
        shift = pltpu.roll(ext, 128 - 8, 2) + pltpu.roll(ext, 128 - 16, 2) + pltpu.roll(ext, 128 - 24, 2)
        wt = jnp.exp2(shift - jnp.max(shift, axis=0, keepdims=True))
        wt = jnp.where((lane >= 64) & (lane < 70), wt, 0.0)
        both[24:32, :] = jnp.sum(ext * wt, axis=0)
        for q in range(3):
            fac = jnp.where(lane < 64, wt[:, :, 64 + q : 65 + q], wt[:, :, 67 + q : 68 + q])
            both[q * 8 : (q + 1) * 8, :] = jnp.sum(x[:, q * 8 : (q + 1) * 8, :] * fac, axis=0)

    low = lanes((8, 128)) < 64
    parts = []
    for q in range(3):
        tot = jnp.where(low, both[24:32, 64 + q : 65 + q], both[24:32, 67 + q : 68 + q])
        parts.append(both[q * 8 : (q + 1) * 8, :] / tot)
    mean = jnp.concatenate(parts, axis=0).astype(bf16)
    for k in range(out_ref.shape[0]):
        out_ref[k] = mean


def merge(parts, copies):
    return pl.pallas_call(
        merge_kernel,
        out_shape=shape((copies, 24, 128)),
        in_specs=[vmem()],
        out_specs=vmem(),
        scratch_shapes=[pltpu.VMEM((32, 128), f32)],
        compiler_params=params(),
        cost_estimate=cost(0, 1 << 20),
        name="merge",
    )(parts)


def latent_kernel(
    pos_ref, g_own, g_oth, pack_own, pack_oth, small,
    wl_own, wl_oth, up_own, up_oth, down_own, down_oth,
    at_ref, b_ref,
    enc, mix, wbuf, sem,
):
    rows = mix.shape[0]
    head = pos_ref[0]
    copies = {}
    for i in (2, 3, 1, 4, 5, 6):
        for k, (src, at) in enumerate(((wl_own, head), (wl_oth, 1 - head))):
            dst = wbuf.at[i - 1, pl.ds(pl.multiple_of(at * HALF, HALF), HALF)]
            copies[i, k] = pltpu.make_async_copy(src.at[i], dst, sem.at[i - 1, k])
            copies[i, k].start()
    for k, (g, pack) in enumerate(((g_own, pack_own), (g_oth, pack_oth))):
        mean = g[...].astype(f32).reshape(GROUPS, 2, 3, 8, 128)
        for p in range(PAIRS):
            cols = slice(p * 128, (p + 1) * 128)
            part = mean[:, p // 3, p % 3].reshape(rows, 128).astype(bf16)
            val = dot(part, block_diag(small[VAL : VAL + 64, cols]))
            enc[k * rows : (k + 1) * rows, cols] = (pack[HALF:, cols].astype(f32) + val).astype(bf16)
    block_in = norm(enc[...].astype(f32)).astype(bf16)

    def proj(x, i):
        for k in range(2):
            copies[i, k].wait()
        return dot(x, wbuf[i - 1])

    keys = proj(block_in, 2).astype(bf16)
    vals = proj(block_in, 3).astype(bf16)
    query = proj(block_in[:rows], 1).astype(bf16)
    ones = jnp.ones((2 * rows, 128), bf16)
    low = lanes((rows, 128)) < 64
    zero = jnp.zeros((rows, 128), bf16)
    for p in range(PAIRS):
        cols = slice(p * 128, (p + 1) * 128)
        qp = query[:, cols]
        both = jnp.concatenate([jnp.where(low, qp, zero), jnp.where(low, zero, qp)], axis=0)
        sc = dot(both, keys[:, cols], NT) * LOG2_SCALE
        ex = jnp.exp2(sc - jnp.max(sc, axis=-1, keepdims=True)).astype(bf16)
        res = dot(ex, jnp.concatenate([vals[:, cols], ones], axis=1))
        res = res[:, :128] / res[:, 128:]
        mix[:, cols] = jnp.where(low, res[:rows], res[rows:]).astype(bf16)
    latent2 = enc[:rows].astype(f32) + proj(mix[...], 4)
    mlp_in = norm(latent2).astype(bf16)
    hidden = []
    for up in (up_own, up_oth):
        x = dot(mlp_in, up[...])
        hid = 0.5 * x * (1.0 + jnp.tanh(math.sqrt(2.0 / math.pi) * (x + 0.044715 * (x * x * x))))
        hidden.append(hid.astype(bf16))
    latents_out = (latent2 + dot(hidden[0], down_own[...]) + dot(hidden[1], down_oth[...])).astype(bf16)
    dec_in = norm(latents_out.astype(f32)).astype(bf16)
    dkeys = proj(dec_in, 5).astype(bf16)
    for p in range(PAIRS):
        cols = slice(p * 128, (p + 1) * 128)
        at_ref[cols, :] = (dot(block_diag(small[QUERY : QUERY + 64, cols]), dkeys[:, cols], NT) * LOG2_SCALE).astype(bf16)
    dvals = proj(dec_in, 6).astype(bf16)
    classes = small[CLASS : CLASS + 16, :]
    lane = lanes(classes.shape)
    none = jnp.zeros_like(classes)
    blocks = [jnp.where((lane >= 64 * h) & (lane < 64 * h + 64), classes, none) for h in range(16)]
    b_ref[...] = dot(dvals, jnp.concatenate(blocks, axis=0), NT).astype(bf16)


def latent_block(pos, g_own, g_oth, pack_own, pack_oth, small, weights):
    rows = pack_own.shape[0] - HALF
    return pl.pallas_call(
        latent_kernel,
        out_shape=(shape((WIDTH, rows)), shape((rows, 256))),
        in_specs=[smem()] + [vmem()] * 5 + [anywhere()] * 2 + [vmem()] * 4,
        out_specs=(vmem(), vmem()),
        scratch_shapes=[
            pltpu.VMEM((2 * rows, WIDTH), bf16),
            pltpu.VMEM((rows, WIDTH), bf16),
            pltpu.VMEM((6, WIDTH, WIDTH), bf16),
            pltpu.SemaphoreType.DMA((6, 2)),
        ],
        compiler_params=params(),
        cost_estimate=cost(6 << 30, 20 << 20, 3 << 20),
        name="latent_block",
    )(pos, g_own, g_oth, pack_own, pack_oth, small, *weights)


DEC_TILE = 1024
TOP_TILE = 128


def decode_kernel(pos_ref, pn_ref, pts_ref, at_own, at_oth, b_own, b_oth, out_ref, pt, amat, bmat):
    share = out_ref.shape[1]
    rows = b_own.shape[0]
    for i in range(share // 128):
        start = pl.multiple_of(pos_ref[0] * share + i * 128, 128)
        blk = pts_ref[:, pl.ds(start, 128)].astype(f32)
        full = jnp.concatenate([blk, jnp.zeros((64, 128), f32)], axis=0)
        pt[i * 128 : (i + 1) * 128, :] = full.T.astype(bf16)
    sub = lax.broadcasted_iota(jnp.int32, (64, 2 * rows), 0)
    lane = lanes((rows, 128))
    worst = jnp.zeros((1, rows), f32)
    for h in range(HEADS):
        amat[h, 64:128, :] = jnp.where((sub >= 3 * h) & (sub < 3 * h + 3), 1.0, 0.0).astype(bf16)
        for k, (a, b) in enumerate(((at_own, b_own), (at_oth, b_oth))):
            part = a[h * 64 : (h + 1) * 64, :]
            amat[h, 0:64, k * rows : (k + 1) * rows] = part
            part = part.astype(f32)
            worst = jnp.maximum(worst, jnp.sum(part * part, axis=0, keepdims=True))
            g = h // 8
            own = (lane >= 16 * (h % 8)) & (lane < 16 * (h % 8) + 16)
            vals = b[:, g * 128 : (g + 1) * 128]
            bmat[h, k * rows : (k + 1) * rows, 0:128] = jnp.where(own, vals, jnp.zeros_like(vals))
            bmat[h, k * rows : (k + 1) * rows, 128:256] = jnp.ones((rows, 128), bf16)

    @pl.when(jnp.max(worst) * pn_ref[0] > SAFE * SAFE)
    def _():
        def tops(j, _):
            at = pl.ds(pl.multiple_of(j * TOP_TILE, TOP_TILE), TOP_TILE)
            pts = pt[at, :]
            new = pts.astype(f32)
            few = lanes((TOP_TILE, 128))
            for h in range(HEADS):
                top = jnp.max(dot(pts, amat[h]), axis=1, keepdims=True)
                for k, part in enumerate(split3(top)):
                    new = jnp.where(few == 64 + 3 * h + k, -part, new)
            pt[at, :] = new.astype(bf16)
            return 0

        lax.fori_loop(0, share // TOP_TILE, tops, 0)

    def block(j, _):
        at = pl.ds(pl.multiple_of(j * DEC_TILE, DEC_TILE), DEC_TILE)
        pts = pt[at, :]
        total = jnp.zeros((DEC_TILE, 128), f32)
        coming = dot(pts, amat[0])
        for h in range(HEADS):
            sc = coming
            if h + 1 < HEADS:
                coming = dot(pts, amat[h + 1])
            res = dot(jnp.exp2(sc).astype(bf16), bmat[h])
            total = total + res[:, :128] / res[:, 128:]
        for turn in (64, 32, 16):
            total = total + pltpu.roll(total, turn, 1)
        out_ref[:, at] = total.T[0:16, :]
        return 0

    lax.fori_loop(0, share // DEC_TILE, block, 0)


def decode(pos, pn, points, at_own, at_oth, b_own, b_oth):
    rows = b_own.shape[0]
    share = points.shape[1] // 2
    return pl.pallas_call(
        decode_kernel,
        out_shape=shape((16, share), f32),
        in_specs=[smem(), smem()] + [vmem()] * 5,
        out_specs=vmem(),
        scratch_shapes=[
            pltpu.VMEM((share, 128), bf16),
            pltpu.VMEM((HEADS, 128, 2 * rows), bf16),
            pltpu.VMEM((HEADS, 2 * rows, 256), bf16),
        ],
        compiler_params=params(),
        cost_estimate=cost(3 << 32, 8 << 20, 12 << 20),
        name="decode",
    )(pos, pn, points, at_own, at_oth, b_own, b_oth)


PARITIES = [list(range(k, OWNERS, 2)) for k in range(2)]


def per_device(
    points, counts, latents_init, enc_key_w, enc_val_w, lat_weights, up_w, down_w, query_w, class_w
):
    swap = [(0, 1), (1, 0)]

    def other(x):
        return lax.ppermute(x, "head", swap)

    pos = lax.axis_index("head").astype(jnp.int32).reshape(1)
    par = (lax.axis_index("pts") & 1).astype(jnp.int32).reshape(1)
    pos, par, lat_weights = lax.optimization_barrier((pos, par, lat_weights))
    pack_own = jnp.concatenate([lat_weights[0], latents_init], axis=0)
    pack_oth = other(pack_own)
    small = jnp.concatenate([enc_key_w, enc_val_w, query_w, class_w.T], axis=0)
    paug, pvt, normed, pn = prepare(counts, points, pack_own, small)
    (pn, pack_oth), late = lax.optimization_barrier(((pn, pack_oth), (lat_weights, up_w, down_w)))
    wl_oth, up_oth, down_oth = [other(w) for w in late]
    away, queries = encode(pos, par, pn, normed, pack_own, pack_oth, small, paug, pvt)
    came = lax.ppermute(away, "pts", [(i, i ^ 1) for i in range(OWNERS)])
    part = pair(encode_rest(queries, paug, pvt), came)

    parts = lax.all_to_all(part, "pts", 0, 0, axis_index_groups=PARITIES)
    g_own = lax.all_to_all(merge(parts, OWNERS), "pts", 0, 0)
    g_oth = other(g_own)

    weights = (lat_weights, wl_oth, up_w, up_oth, down_w, down_oth)
    at_own, b_own = latent_block(pos, g_own, g_oth, pack_own, pack_oth, small, weights)
    return decode(pos, pn, points, at_own, other(at_own), b_own, other(b_own))


def solution(mesh):
    placed = (
        P(None, "pts"),
        P("pts"),
        P("head", None),
        P(),
        P(),
        P(None, "head", None),
        P(None, "head"),
        P("head", None),
        P(),
        P(),
    )
    return jax.shard_map(
        per_device, mesh=mesh, in_specs=placed, out_specs=P(None, ("pts", "head")), check_vma=False
    )
```

```python
import math

import jax
import jax.numpy as jnp
from jax import lax
from jax.experimental import pallas as pl
from jax.experimental.pallas import tpu as pltpu
from jax.sharding import PartitionSpec as P

HEADS = 12
HSIZE = 64
WIDTH = HEADS * HSIZE
PAIRS = HEADS // 2
HALF = WIDTH // 2
KEY, VAL, QUERY, CLASS = 0, 64, 128, 192
OWNERS = 64
GROUPS = 32
LOG2_SCALE = HSIZE ** -0.5 * math.log2(math.e)
SAFE = 64.0
DEAD = -1e30

f32 = jnp.float32
bf16 = jnp.bfloat16
NT = (((1,), (1,)), ((), ()))
NN = (((1,), (0,)), ((), ()))


def dot(a, b, dims=NN):
    return lax.dot_general(a, b, dims, preferred_element_type=f32)


def norm(v):
    mean = jnp.mean(v, axis=-1, keepdims=True)
    cent = v - mean
    var = jnp.mean(cent * cent, axis=-1, keepdims=True)
    return cent * lax.rsqrt(var + 1e-05)


def split3(v):
    hi = v.astype(bf16).astype(f32)
    mid = (v - hi).astype(bf16).astype(f32)
    lo = (v - hi - mid).astype(bf16).astype(f32)
    return hi, mid, lo


def lanes(shape):
    return lax.broadcasted_iota(jnp.int32, shape, len(shape) - 1)


def block_diag(pair):
    lane = lanes(pair.shape)
    zero = jnp.zeros_like(pair)
    return jnp.concatenate([jnp.where(lane < 64, pair, zero), jnp.where(lane >= 64, pair, zero)], axis=0)


def vmem():
    return pl.BlockSpec(memory_space=pltpu.VMEM)


def smem():
    return pl.BlockSpec(memory_space=pltpu.SMEM)


def anywhere():
    return pl.BlockSpec(memory_space=pl.ANY)


def shape(dims, dtype=bf16):
    return jax.ShapeDtypeStruct(dims, dtype)


def params(mib=28):
    return pltpu.CompilerParams(vmem_limit_bytes=mib << 20)


def cost(flops, size, exps=0):
    return pl.CostEstimate(flops=flops, bytes_accessed=size, transcendentals=exps)


def prepare_kernel(count_ref, pts_ref, pack_ref, before, paug, pvt, normed, pn_ref):
    slots = pts_ref.shape[1]
    count = count_ref[0]
    sub = lax.broadcasted_iota(jnp.int32, (64, slots), 0)
    col = lanes((64, slots))
    ext = jnp.where(sub < 3, 1.0, jnp.where((sub == 3) & (col >= count), DEAD, 0.0))
    paug[0:64, :] = pts_ref[...]
    paug[64:128, :] = ext.astype(bf16)
    for i in range(slots // 128):
        blk = pts_ref[:, i * 128 : (i + 1) * 128].astype(f32)
        full = jnp.concatenate([blk, jnp.ones((64, 128), f32)], axis=0)
        pvt[i * 128 : (i + 1) * 128, :] = full.T.astype(bf16)
    normed[...] = norm(pack_ref[HALF:, :].astype(f32)).astype(bf16)
    pall = pts_ref[...].astype(f32)
    pn_ref[0] = jnp.max(jnp.sum(pall * pall, axis=0, keepdims=True))


def prepare(count, points, pack, before):
    slots = points.shape[1]
    return pl.pallas_call(
        prepare_kernel,
        out_shape=(shape((128, slots)), shape((slots, 128)), shape((pack.shape[0] - HALF, WIDTH)), shape((1,), f32)),
        in_specs=[smem(), vmem(), vmem(), anywhere()],
        out_specs=(vmem(), vmem(), vmem(), smem()),
        compiler_params=params(),
        cost_estimate=cost(0, 6 << 20),
        name="prepare",
    )(count, points, pack, before)


PT_TURN = 4 * 512
TOP_ROWS = 256
PT_TILE = 512


def encode_kernel(pos_ref, par_ref, pn_ref, normed, pack_own, pack_oth, small, paug, pvt, out_ref, q_ref, qf, qaug, acc):
    rows = qaug.shape[1]
    slots = paug.shape[1]
    keep = par_ref[0]

    lo, hi = normed[:, :HALF], normed[:, HALF:]
    first = pos_ref[0] == 0
    equery = dot(jnp.where(first, lo, hi), pack_own[:HALF, :]) + dot(jnp.where(first, hi, lo), pack_oth[:HALF, :])
    equery = equery.astype(bf16)
    lane8 = lanes((GROUPS, 8, 128))
    aug = jnp.where(lane8 == 67, 1.0, 0.0)
    for p in range(PAIRS):
        cols = slice(p * 128, (p + 1) * 128)
        x = dot(equery[:, cols], block_diag(small[KEY : KEY + 64, cols]), NT) * LOG2_SCALE
        x8 = x.reshape(GROUPS, 8, 128)
        y8 = pltpu.roll(x, 64, 1).reshape(GROUPS, 8, 128)
        s, q = p // 3, p % 3
        qf[s, 0, :, q] = jnp.where(lane8 < 64, x8, aug)
        qf[s, 1, :, q] = jnp.where(lane8 < 64, y8, aug)
    qall = qf[...].reshape(2 * rows, 128)
    qaug[...] = qall.astype(bf16).reshape(2, rows, 128)

    sub = lax.broadcasted_iota(jnp.int32, (128, 128), 0)
    sums = dot((qall * qall).astype(bf16), jnp.where(sub < 64, 1.0, 0.0).astype(bf16))
    shifted = jnp.max(sums) * pn_ref[0] > SAFE * SAFE

    @pl.when(shifted)
    def _():
        def tile(t, _):
            per = rows // TOP_ROWS
            at = pl.ds(pl.multiple_of(lax.rem(t, per) * TOP_ROWS, TOP_ROWS), TOP_ROWS)
            qt = qaug[t // per, at, :]

            def chunk(j, top):
                start = pl.multiple_of(j * PT_TILE, PT_TILE)
                sc = dot(qt, paug[:, pl.ds(start, PT_TILE)])
                return jnp.maximum(top, jnp.max(sc, axis=1, keepdims=True))

            top = lax.fori_loop(0, slots // PT_TILE, chunk, jnp.full((TOP_ROWS, 1), DEAD, f32))
            hi, mid, lo = split3(top)
            lane = lanes((TOP_ROWS, 128))
            shift = jnp.where(lane == 64, hi, jnp.where(lane == 65, mid, lo))
            same = (lane < 64) | (lane > 66)
            qaug[t // per, at, :] = jnp.where(same, qt.astype(f32), -shift).astype(bf16)
            return 0

        lax.fori_loop(0, 2 * rows // TOP_ROWS, tile, 0)

    q_ref[...] = qaug[keep]
    attend(qaug.at[1 - keep], paug, pvt, out_ref, acc)


def attend(q_ref, paug, pvt, out_ref, acc):
    rows = q_ref.shape[0]
    slots = paug.shape[1]
    qt = q_ref[...]
    acc[...] = jnp.zeros(acc.shape, f32)

    def turn(t, _):
        total = acc[...]
        for j in range(PT_TURN // PT_TILE):
            cols = pl.ds(pl.multiple_of(t * PT_TURN + j * PT_TILE, PT_TILE), PT_TILE)
            ex = jnp.exp2(dot(qt, paug[:, cols])).astype(bf16)
            total = total + dot(ex, pvt[cols, :])
        acc[...] = total
        return 0

    lax.fori_loop(0, slots // PT_TURN, turn, 0)

    sums = acc[...].reshape(2, GROUPS, 3, 8, 128)
    turned = pltpu.roll(acc[rows // 2 :, :], 64, 1).reshape(GROUPS, 3, 8, 128)
    lane = lanes((GROUPS, 8, 128))
    parts = [jnp.where(lane < 64, sums[0, :, q], turned[:, q]) for q in range(3)]
    extra = jnp.zeros((GROUPS, 8, 128), f32)
    for e in range(2):
        for q in range(3):
            extra = jnp.where(lane == 64 + 3 * e + q, sums[e, :, q], extra)
    out_ref[...] = jnp.concatenate(parts + [extra], axis=1).astype(bf16)

    shifts = -q_ref[...].astype(f32)
    at = lanes(shifts.shape)
    shifted = jnp.max(jnp.where((at >= 64) & (at < 67), jnp.abs(shifts), 0.0)) > 0.0

    @pl.when(shifted)
    def _():
        tiles = shifts.reshape(2, GROUPS, 3, 8, 128)
        more = extra
        for e in range(2):
            for q in range(3):
                for k in range(3):
                    one = tiles[e, :, q, :, 64 + k : 65 + k]
                    more = jnp.where(lane == 72 + 8 * k + 3 * e + q, one, more)
        out_ref[...] = jnp.concatenate(parts + [more], axis=1).astype(bf16)


def encode(pos, par, pn, normed, pack_own, pack_oth, small, paug, pvt):
    slots = paug.shape[1]
    rows = normed.shape[0] * HEADS // 2
    return pl.pallas_call(
        encode_kernel,
        out_shape=(shape((GROUPS, 32, 128)), shape((rows, 128))),
        in_specs=[smem()] * 3 + [vmem()] * 6,
        out_specs=(vmem(), vmem()),
        scratch_shapes=[
            pltpu.VMEM((2, 2, GROUPS, 3, 8, 128), f32),
            pltpu.VMEM((2, rows, 128), bf16),
            pltpu.VMEM((rows, 128), f32),
        ],
        compiler_params=params(),
        cost_estimate=cost(rows * slots * 1024, 6 << 20, rows * slots),
        name="encode",
    )(pos, par, pn, normed, pack_own, pack_oth, small, paug, pvt)


def encode_rest(queries, paug, pvt):
    rows, slots = queries.shape[0], paug.shape[1]
    return pl.pallas_call(
        attend,
        out_shape=shape((GROUPS, 32, 128)),
        in_specs=[vmem()] * 3,
        out_specs=vmem(),
        scratch_shapes=[pltpu.VMEM((rows, 128), f32)],
        compiler_params=params(),
        cost_estimate=cost(rows * slots * 1024, 6 << 20, rows * slots),
        name="encode_rest",
    )(queries, paug, pvt)


def pair_kernel(x_ref, y_ref, out_ref):
    xs = [x_ref[...].astype(f32), y_ref[...].astype(f32)]
    exts = [x[:, 24:32, :] for x in xs]
    lane = lanes(exts[0].shape)
    inside = (lane >= 72) & (lane < 96)
    flag = jnp.max(jnp.where(inside, jnp.maximum(jnp.abs(exts[0]), jnp.abs(exts[1])), 0.0))
    out_ref[...] = (xs[0] + xs[1]).astype(bf16)

    @pl.when(flag > 0.0)
    def _():
        shifts = [pltpu.roll(e, 128 - 8, 2) + pltpu.roll(e, 128 - 16, 2) + pltpu.roll(e, 128 - 24, 2) for e in exts]
        top = jnp.maximum(shifts[0], shifts[1])
        total = jnp.zeros(lane.shape, f32)
        parts = [jnp.zeros(lane.shape, f32) for _ in range(3)]
        here = (lane >= 64) & (lane < 70)
        for x, e, s in zip(xs, exts, shifts):
            wt = jnp.where(here, jnp.exp2(s - top), 0.0)
            total = total + e * wt
            for q in range(3):
                fac = jnp.where(lane < 64, wt[:, :, 64 + q : 65 + q], wt[:, :, 67 + q : 68 + q])
                parts[q] = parts[q] + x[:, q * 8 : (q + 1) * 8, :] * fac
        for k, part in enumerate(split3(jnp.where(here, top, 0.0))):
            total = total + pltpu.roll(part, 8 * (k + 1), 2)
        out_ref[...] = jnp.concatenate(parts + [total], axis=1).astype(bf16)


def pair(x, y):
    return pl.pallas_call(
        pair_kernel,
        out_shape=shape(x.shape),
        in_specs=[vmem()] * 2,
        out_specs=vmem(),
        compiler_params=params(),
        cost_estimate=cost(0, 1 << 20),
        name="pair",
    )(x, y)


def merge_kernel(x_ref, out_ref, both):
    x = x_ref[...].astype(f32)
    ext = x[:, 24:32, :]
    lane = lanes(ext.shape)
    flag = jnp.max(jnp.where((lane >= 72) & (lane < 96), jnp.abs(ext), 0.0))
    both[...] = jnp.sum(x, axis=0)

    @pl.when(flag > 0.0)
    def _():
        shift = pltpu.roll(ext, 128 - 8, 2) + pltpu.roll(ext, 128 - 16, 2) + pltpu.roll(ext, 128 - 24, 2)
        wt = jnp.exp2(shift - jnp.max(shift, axis=0, keepdims=True))
        wt = jnp.where((lane >= 64) & (lane < 70), wt, 0.0)
        both[24:32, :] = jnp.sum(ext * wt, axis=0)
        for q in range(3):
            fac = jnp.where(lane < 64, wt[:, :, 64 + q : 65 + q], wt[:, :, 67 + q : 68 + q])
            both[q * 8 : (q + 1) * 8, :] = jnp.sum(x[:, q * 8 : (q + 1) * 8, :] * fac, axis=0)

    low = lanes((8, 128)) < 64
    parts = []
    for q in range(3):
        tot = jnp.where(low, both[24:32, 64 + q : 65 + q], both[24:32, 67 + q : 68 + q])
        parts.append(both[q * 8 : (q + 1) * 8, :] / tot)
    mean = jnp.concatenate(parts, axis=0).astype(bf16)
    for k in range(out_ref.shape[0]):
        out_ref[k] = mean


def merge(parts, copies):
    return pl.pallas_call(
        merge_kernel,
        out_shape=shape((copies, 24, 128)),
        in_specs=[vmem()],
        out_specs=vmem(),
        scratch_shapes=[pltpu.VMEM((32, 128), f32)],
        compiler_params=params(),
        cost_estimate=cost(0, 1 << 20),
        name="merge",
    )(parts)


def latent_kernel(
    pos_ref, g_own, g_oth, pack_own, pack_oth, small,
    wl_own, wl_oth, up_own, up_oth, down_own, down_oth,
    at_ref, b_ref,
    enc, mix,
):
    rows = mix.shape[0]
    head = pos_ref[0]
    first = head == 0
    for k, (g, pack) in enumerate(((g_own, pack_own), (g_oth, pack_oth))):
        mean = g[...].astype(f32).reshape(GROUPS, 2, 3, 8, 128)
        for p in range(PAIRS):
            cols = slice(p * 128, (p + 1) * 128)
            part = mean[:, p // 3, p % 3].reshape(rows, 128).astype(bf16)
            val = dot(part, block_diag(small[VAL : VAL + 64, cols]))
            enc[k * rows : (k + 1) * rows, cols] = (pack[HALF:, cols].astype(f32) + val).astype(bf16)
    block_in = norm(enc[...].astype(f32)).astype(bf16)

    def proj(x, i):
        lo, hi = x[:, :HALF], x[:, HALF:]
        return dot(jnp.where(first, lo, hi), wl_own[i]) + dot(jnp.where(first, hi, lo), wl_oth[i])

    keys = proj(block_in, 2).astype(bf16)
    vals = proj(block_in, 3).astype(bf16)
    query = proj(block_in[:rows], 1).astype(bf16)
    ones = jnp.ones((2 * rows, 128), bf16)
    low = lanes((rows, 128)) < 64
    zero = jnp.zeros((rows, 128), bf16)
    for p in range(PAIRS):
        cols = slice(p * 128, (p + 1) * 128)
        qp = query[:, cols]
        both = jnp.concatenate([jnp.where(low, qp, zero), jnp.where(low, zero, qp)], axis=0)
        sc = dot(both, keys[:, cols], NT) * LOG2_SCALE
        ex = jnp.exp2(sc - jnp.max(sc, axis=-1, keepdims=True)).astype(bf16)
        res = dot(ex, jnp.concatenate([vals[:, cols], ones], axis=1))
        res = res[:, :128] / res[:, 128:]
        mix[:, cols] = jnp.where(low, res[:rows], res[rows:]).astype(bf16)
    latent2 = enc[:rows].astype(f32) + proj(mix[...], 4)
    mlp_in = norm(latent2).astype(bf16)
    hidden = []
    for up in (up_own, up_oth):
        x = dot(mlp_in, up[...])
        hid = 0.5 * x * (1.0 + jnp.tanh(math.sqrt(2.0 / math.pi) * (x + 0.044715 * (x * x * x))))
        hidden.append(hid.astype(bf16))
    latents_out = (latent2 + dot(hidden[0], down_own[...]) + dot(hidden[1], down_oth[...])).astype(bf16)
    dec_in = norm(latents_out.astype(f32)).astype(bf16)
    dkeys = proj(dec_in, 5).astype(bf16)
    for p in range(PAIRS):
        cols = slice(p * 128, (p + 1) * 128)
        at_ref[cols, :] = (dot(block_diag(small[QUERY : QUERY + 64, cols]), dkeys[:, cols], NT) * LOG2_SCALE).astype(bf16)
    dvals = proj(dec_in, 6).astype(bf16)
    classes = small[CLASS : CLASS + 16, :]
    lane = lanes(classes.shape)
    none = jnp.zeros_like(classes)
    blocks = [jnp.where((lane >= 64 * h) & (lane < 64 * h + 64), classes, none) for h in range(16)]
    b_ref[...] = dot(dvals, jnp.concatenate(blocks, axis=0), NT).astype(bf16)


def latent_block(pos, g_own, g_oth, pack_own, pack_oth, small, weights):
    rows = pack_own.shape[0] - HALF
    return pl.pallas_call(
        latent_kernel,
        out_shape=(shape((WIDTH, rows)), shape((rows, 256))),
        in_specs=[smem()] + [vmem()] * 11,
        out_specs=(vmem(), vmem()),
        scratch_shapes=[
            pltpu.VMEM((2 * rows, WIDTH), bf16),
            pltpu.VMEM((rows, WIDTH), bf16),
        ],
        compiler_params=params(),
        cost_estimate=cost(6 << 30, 20 << 20, 3 << 20),
        name="latent_block",
    )(pos, g_own, g_oth, pack_own, pack_oth, small, *weights)


DEC_TILE = 1024
TOP_TILE = 128


def decode_kernel(pos_ref, pn_ref, pts_ref, at_own, at_oth, b_own, b_oth, out_ref, pt, amat, bmat):
    share = out_ref.shape[1]
    rows = b_own.shape[0]
    for i in range(share // 128):
        start = pl.multiple_of(pos_ref[0] * share + i * 128, 128)
        blk = pts_ref[:, pl.ds(start, 128)].astype(f32)
        full = jnp.concatenate([blk, jnp.zeros((64, 128), f32)], axis=0)
        pt[i * 128 : (i + 1) * 128, :] = full.T.astype(bf16)
    sub = lax.broadcasted_iota(jnp.int32, (64, 2 * rows), 0)
    lane = lanes((rows, 128))
    worst = jnp.zeros((1, rows), f32)
    for h in range(HEADS):
        amat[h, 64:128, :] = jnp.where((sub >= 3 * h) & (sub < 3 * h + 3), 1.0, 0.0).astype(bf16)
        for k, (a, b) in enumerate(((at_own, b_own), (at_oth, b_oth))):
            part = a[h * 64 : (h + 1) * 64, :]
            amat[h, 0:64, k * rows : (k + 1) * rows] = part
            part = part.astype(f32)
            worst = jnp.maximum(worst, jnp.sum(part * part, axis=0, keepdims=True))
            g = h // 8
            own = (lane >= 16 * (h % 8)) & (lane < 16 * (h % 8) + 16)
            vals = b[:, g * 128 : (g + 1) * 128]
            bmat[h, k * rows : (k + 1) * rows, 0:128] = jnp.where(own, vals, jnp.zeros_like(vals))
            bmat[h, k * rows : (k + 1) * rows, 128:256] = jnp.ones((rows, 128), bf16)

    @pl.when(jnp.max(worst) * pn_ref[0] > SAFE * SAFE)
    def _():
        def tops(j, _):
            at = pl.ds(pl.multiple_of(j * TOP_TILE, TOP_TILE), TOP_TILE)
            pts = pt[at, :]
            new = pts.astype(f32)
            few = lanes((TOP_TILE, 128))
            for h in range(HEADS):
                top = jnp.max(dot(pts, amat[h]), axis=1, keepdims=True)
                for k, part in enumerate(split3(top)):
                    new = jnp.where(few == 64 + 3 * h + k, -part, new)
            pt[at, :] = new.astype(bf16)
            return 0

        lax.fori_loop(0, share // TOP_TILE, tops, 0)

    def block(j, _):
        at = pl.ds(pl.multiple_of(j * DEC_TILE, DEC_TILE), DEC_TILE)
        pts = pt[at, :]
        total = jnp.zeros((DEC_TILE, 128), f32)
        coming = dot(pts, amat[0])
        for h in range(HEADS):
            sc = coming
            if h + 1 < HEADS:
                coming = dot(pts, amat[h + 1])
            res = dot(jnp.exp2(sc).astype(bf16), bmat[h])
            total = total + res[:, :128] / res[:, 128:]
        for turn in (64, 32, 16):
            total = total + pltpu.roll(total, turn, 1)
        out_ref[:, at] = total.T[0:16, :]
        return 0

    lax.fori_loop(0, share // DEC_TILE, block, 0)


def decode(pos, pn, points, at_own, at_oth, b_own, b_oth):
    rows = b_own.shape[0]
    share = points.shape[1] // 2
    return pl.pallas_call(
        decode_kernel,
        out_shape=shape((16, share), f32),
        in_specs=[smem(), smem()] + [vmem()] * 5,
        out_specs=vmem(),
        scratch_shapes=[
            pltpu.VMEM((share, 128), bf16),
            pltpu.VMEM((HEADS, 128, 2 * rows), bf16),
            pltpu.VMEM((HEADS, 2 * rows, 256), bf16),
        ],
        compiler_params=params(),
        cost_estimate=cost(3 << 32, 8 << 20, 12 << 20),
        name="decode",
    )(pos, pn, points, at_own, at_oth, b_own, b_oth)


PARITIES = [list(range(k, OWNERS, 2)) for k in range(2)]


def per_device(
    points, counts, latents_init, enc_key_w, enc_val_w, lat_weights, up_w, down_w, query_w, class_w
):
    swap = [(0, 1), (1, 0)]

    def other(x):
        return lax.ppermute(x, "head", swap)

    pos = lax.axis_index("head").astype(jnp.int32).reshape(1)
    par = (lax.axis_index("pts") & 1).astype(jnp.int32).reshape(1)
    pos, par, lat_weights = lax.optimization_barrier((pos, par, lat_weights))
    pack_own = jnp.concatenate([lat_weights[0], latents_init], axis=0)
    pack_oth = other(pack_own)
    small = jnp.concatenate([enc_key_w, enc_val_w, query_w, class_w.T], axis=0)
    paug, pvt, normed, pn = prepare(counts, points, pack_own, small)
    (pn, pack_oth), late = lax.optimization_barrier(((pn, pack_oth), (lat_weights, up_w, down_w)))
    wl_oth, up_oth, down_oth = [other(w) for w in late]
    away, queries = encode(pos, par, pn, normed, pack_own, pack_oth, small, paug, pvt)
    came = lax.ppermute(away, "pts", [(i, i ^ 1) for i in range(OWNERS)])
    part = pair(encode_rest(queries, paug, pvt), came)

    parts = lax.all_to_all(part, "pts", 0, 0, axis_index_groups=PARITIES)
    g_own = lax.all_to_all(merge(parts, OWNERS), "pts", 0, 0)
    g_oth = other(g_own)

    weights = (lat_weights, wl_oth, up_w, up_oth, down_w, down_oth)
    at_own, b_own = latent_block(pos, g_own, g_oth, pack_own, pack_oth, small, weights)
    return decode(pos, pn, points, at_own, other(at_own), b_own, other(b_own))


def solution(mesh):
    placed = (
        P(None, "pts"),
        P("pts"),
        P("head", None),
        P(),
        P(),
        P(None, "head", None),
        P(None, "head"),
        P("head", None),
        P(),
        P(),
    )
    return jax.shard_map(
        per_device, mesh=mesh, in_specs=placed, out_specs=P(None, ("pts", "head")), check_vma=False
    )
```
